512 devices in a mesh: grp: 64 (over y, x, z_hi), tp: 8 (over z_lo, core).
Axes of the slice: x: 4, y: 4, z: 16 (z_hi: 4, z_lo: 4; z = z_hi * 4 + z_lo), core: 2. Of those that a mesh axis runs over, the one named last changes fastest.
Arguments:
- tokens: bfloat16 [32768, 6144], P('grp', 'tp'), may hold values from -60 to 60
- gain: float32 [6144], P('tp'), may hold values from 0.1 to 1.9
- kv_weight: bfloat16 [6144, 2048], P('tp'), may hold values from -0.078125 to 0.078125
- kv_bias: float32 [2048], P('tp'), may hold values from -3 to 3
- lengths: int32 [64, 64], replicated, may hold values from 1 to 16, 512 in all within a row
- dest: int32 [64, 64], replicated, may hold values from 0 to 63, each once within a row
- queries: bfloat16 [64, 64, 2, 8192], P('grp', None, None, 'tp'), may hold values from -16 to 16
- old_cache: bfloat16 [64, 64, 16, 2048], P('grp', None, None, 'tp'), may hold values from -4 to 4
- new_kv: bfloat16 [64, 64, 2, 2048], P('grp', None, None, 'tp'), may hold values from -5 to 5
Outputs:
- attended: bfloat16 [64, 64, 2, 8192], P('grp', None, None, 'tp')
The draws below stay inside these ranges and needn't reach their ends.
Inputs may be any that keep to these rules, and one draw needn't show every extreme that they name: `lengths`: row g lists the prompt rows of prefill group g's requests in block order; each row sums to 512 and its largest entry is exactly 16. `dest`: each row is a permutation of the decode groups, so each decode group receives exactly one request from every prefill group.
All inputs are finite; a program needn't handle non-finite values.
Results may differ from the reference program's by a relative error of at most 0.0058.
Values may be sent and summed in bfloat16 or wider, within the bound.
A program may use at most 64 MiB of HBM per device.

```python
import math
import jax
import jax.numpy as jnp
import numpy as np
from jax import lax

D = 6144
HD = 128
KVH = 8
QH = 64
SLOT = 16
CACHED = 16
STEPS = 2
REQS = 64
SPAN = 512
KVW = 2048
QPK = 8
N_GRP = 64


def draw_tokens(key, part):
    key = jax.random.fold_in(key, 23)
    shape = (N_GRP * SPAN, D)
    column_level = jnp.arange(D, dtype=jnp.float32) / D
    base = jnp.clip(jax.random.normal(key, shape, jnp.float32), -5.0, 5.0)
    value = base * jnp.exp(0.5 * math.log(3.0) * column_level)[None, :]
    return value.astype(jnp.bfloat16)


def draw_old_cache(key, part):
    key = jax.random.fold_in(key, 21)
    shape = (N_GRP, N_GRP, CACHED, KVW)
    value = jnp.clip(jax.random.normal(key, shape, jnp.float32), -4.0, 4.0)
    return value.astype(jnp.bfloat16)


def draw_queries(key, part):
    key = jax.random.fold_in(key, 22)
    shape = (N_GRP, N_GRP, STEPS, QH * HD)
    value = jnp.clip(jax.random.normal(key, shape, jnp.float32), -5.0, 5.0)
    return value.astype(jnp.bfloat16)


def block_scale(stream_key, extent, shards, low, largest):
    def one(position, parts):
        heights = jax.random.uniform(jax.random.fold_in(jax.random.fold_in(stream_key, 6), position), (parts,), jnp.float32, low / len(shards), largest / len(shards))
        return jnp.repeat(jnp.exp(heights), extent[position] // parts).reshape((-1,) + (1,) * (len(extent) - position - 1))

    factor_of = one(*shards[0])
    for cut in shards[1:]:
        factor_of = factor_of * one(*cut)
    return factor_of


def split_up(count, total, most, skew):
    portions = [(1 << 20) // math.isqrt(standing ** skew) + 1 for standing in range(2, count + 1)]
    spare, holding = total - most - (count - 1), [1] * (count - 1)
    while spare > 0:
        free = [i for i in range(count - 1) if holding[i] < most]
        mass, budget = sum([portions[i] for i in free]), spare
        for i in free:
            extra = min(most - holding[i], max(1, budget * portions[i] // mass), spare)
            holding[i] = holding[i] + extra
            spare = spare - extra
    return np.array([most] + holding)


def ragged(stream_key, amount, total, bound, slope):
    if amount == 2:
        one = jax.random.randint(stream_key, (), max(1, total - bound), min(bound, total - 1) + 1)
        return jnp.stack([one, total - one])
    sizes = jnp.asarray(split_up(amount, total, bound, slope), jnp.int32)
    twos = (amount - 1) // 2
    source_of, taker = sizes[1:1 + 2 * twos:2], sizes[2:2 + 2 * twos:2]
    margin = jnp.minimum(source_of - 1, bound - taker)
    moved = jax.random.randint(jax.random.fold_in(stream_key, 1), (twos,), 0, 1 << 20) % (margin + 1)
    sizes = sizes.at[1:1 + 2 * twos:2].set(source_of - moved).at[2:2 + 2 * twos:2].set(taker + moved)
    return sizes[jax.random.permutation(jax.random.fold_in(stream_key, 2), amount)]


def bell_draw(own_key, dims, spread, most, shards=(), kind=jnp.bfloat16):
    factor_of = block_scale(own_key, dims, shards, -0.22, 0.18) if shards else 1.0
    drawn = jax.random.normal(own_key, dims, jnp.float32) * spread * factor_of
    return jnp.minimum(jnp.maximum(drawn, -most), most).astype(kind)


def setup_inputs(seed: int = 0) -> dict:
    seeds = jax.random.split(jax.random.key(seed), 10)
    tokens = draw_tokens(jax.random.fold_in(seeds[9], 71), 0)
    gain = jnp.clip(1.0 + 0.18 * jax.random.normal(seeds[1], (D,), jnp.float32), 0.1, 1.9)
    kv_weight = bell_draw(seeds[2], (D, KVW), D ** -0.5, 0.078125, ((0, 8),))
    kv_bias = bell_draw(seeds[3], (KVW,), 0.5, 3.0, ((0, 8),), jnp.float32)
    lengths = jax.vmap(lambda own: ragged(own, REQS, SPAN, SLOT, 2))(jax.random.split(seeds[4], N_GRP)).reshape((N_GRP, REQS)).astype(jnp.int32)
    dest = jax.vmap(lambda own: jax.random.permutation(own, N_GRP))(jax.random.split(seeds[5], N_GRP)).reshape((N_GRP, REQS)).astype(jnp.int32)
    queries = draw_queries(jax.random.fold_in(seeds[9], 71), 0)
    old_cache = draw_old_cache(jax.random.fold_in(seeds[9], 71), 0)
    new_kv = bell_draw(seeds[8], (N_GRP, N_GRP, STEPS, KVW), 1.0, 5.0, ((0, 64), (3, 8)))
    return {"tokens": tokens, "gain": gain, "kv_weight": kv_weight, "kv_bias": kv_bias, "lengths": lengths, "dest": dest, "queries": queries, "old_cache": old_cache, "new_kv": new_kv}


EPSILON = 1e-06
THETA = 1000000.0

def rotary(rotated_in, positions):
    half_width = rotated_in.shape[-1] // 2
    frequency = THETA ** (-2.0 * jnp.arange(half_width, dtype=jnp.float32) / HD)
    angles = positions[:, None, None] * frequency[None, None, :]
    cosine = jnp.cos(angles)
    sine_part = jnp.sin(angles)
    first_half = rotated_in[..., :half_width]
    second_half = rotated_in[..., half_width:]
    return jnp.concatenate([first_half * cosine - second_half * sine_part, second_half * cosine + first_half * sine_part], axis=-1)

def group_kv(block, span_lengths, gain, kv_weight, kv_bias):
    floats = block.astype(jnp.float32)
    inv_rms = lax.rsqrt(lax.optimization_barrier(jnp.mean(floats * floats, axis=1)) + EPSILON)
    normed = (floats * inv_rms[:, None] * gain[None, :]).astype(jnp.bfloat16)
    projected = jnp.dot(normed, kv_weight, preferred_element_type=jnp.float32) + kv_bias[None, :]
    row_index = jnp.arange(SPAN, dtype=jnp.int32)
    row_ends = jnp.cumsum(span_lengths).astype(jnp.int32)
    starts = row_ends - span_lengths
    owning = lax.optimization_barrier(jnp.sum((row_ends[None, :] <= row_index[:, None]).astype(jnp.int32), axis=1))
    request_ids = jnp.arange(REQS, dtype=jnp.int32)
    first_row = lax.optimization_barrier(jnp.sum(jnp.where(owning[:, None] == request_ids[None, :], starts[None, :], 0), axis=1))
    positions = (CACHED + row_index - first_row).astype(jnp.float32)
    parted = projected.reshape(SPAN, KVH, 2, HD)
    rotated_keys = rotary(parted[:, :, 0, :], positions)
    joined = jnp.stack([rotated_keys, parted[:, :, 1, :]], axis=2)
    return joined.reshape(SPAN, KVW).astype(jnp.bfloat16)

def attend(query_block, old_rows, new_rows, span_rows, live_rows):
    sources = query_block.shape[0]
    query_floats = query_block.reshape(sources, STEPS, KVH, QPK, HD).astype(jnp.float32)
    all_rows = jnp.concatenate([old_rows, span_rows, new_rows], axis=1)
    all_rows = all_rows.reshape(sources, CACHED + SLOT + STEPS, KVH, 2, HD).astype(jnp.float32)
    scores = jnp.einsum('sthgd,srhd->sthgr', query_floats, all_rows[:, :, :, 0, :]) / math.sqrt(HD)
    slot_index = jnp.arange(SLOT, dtype=jnp.int32)
    span_mask = slot_index[None, :] < live_rows[:, None]
    step_index = jnp.arange(STEPS, dtype=jnp.int32)
    new_mask = step_index[None, :] <= step_index[:, None]
    full_mask = jnp.concatenate([jnp.ones((sources, STEPS, CACHED), dtype=jnp.bool_), jnp.broadcast_to(span_mask[:, None, :], (sources, STEPS, SLOT)), jnp.broadcast_to(new_mask[None, :, :], (sources, STEPS, STEPS))], axis=2)
    scores = jnp.where(full_mask[:, :, None, None, :], scores, -1e+30)
    row_max = lax.optimization_barrier(jnp.max(scores, axis=-1, keepdims=True))
    weights = jnp.exp(scores - row_max)
    probabilities = (weights / lax.optimization_barrier(jnp.sum(weights, axis=-1, keepdims=True))).astype(jnp.bfloat16)
    output = jnp.einsum('sthgr,srhd->sthgd', probabilities.astype(jnp.float32), all_rows[:, :, :, 1, :])
    return output.reshape(sources, STEPS, QH * HD).astype(jnp.bfloat16)

def reference(tokens, gain, kv_weight, kv_bias, lengths, dest, queries, old_cache, new_kv):
    blocks = tokens.reshape(N_GRP, SPAN, D)
    handed = lax.map(lambda operands: group_kv(operands[0], operands[1], gain, kv_weight, kv_bias), (blocks, lengths))
    padded = jnp.concatenate([handed, jnp.zeros((N_GRP, SLOT, KVW), jnp.bfloat16)], axis=1)
    all_starts = (jnp.cumsum(lengths, axis=1) - lengths).astype(jnp.int32)

    def decode_group(operands):
        target, query_block, old_rows, new_rows = operands
        picked = dest == target
        first_rows = lax.optimization_barrier(jnp.sum(jnp.where(picked, all_starts, 0), axis=1)).astype(jnp.int32)
        live_rows = lax.optimization_barrier(jnp.sum(jnp.where(picked, lengths, 0), axis=1)).astype(jnp.int32)
        span_rows = jax.vmap(lambda source, offset: lax.dynamic_slice_in_dim(source, offset, SLOT, 0))(padded, first_rows)
        return attend(query_block, old_rows, new_rows, span_rows, live_rows)
    return lax.map(decode_group, (jnp.arange(N_GRP, dtype=jnp.int32), queries, old_cache, new_kv))
```

```python
import functools
import math

import jax
import jax.numpy as jnp
import numpy as np
from jax import lax
from jax.experimental import pallas as pl
from jax.experimental.pallas import tpu as pltpu
from jax.sharding import PartitionSpec as P

D = 6144
HD = 128
SLOT = 16
CACHED = 16
STEPS = 2
KVW = 2048
QPK = 8
EPSILON = 1e-06
THETA = 1000000.0

ROWS = 512
FEATS = 768
GRP = 64
TP = 8
CHIPS = 4
WIDTH = 256
HALF = ROWS // 2
SLOTS = GRP * SLOT
MESH = pl.DeviceIdType.MESH
F32 = jnp.float32
BF16 = jnp.bfloat16
NT = (((1,), (1,)), ((), ()))
NN = (((1,), (0,)), ((), ()))


def dot(a, b, dims=NN):
    return lax.dot_general(a, b, dims, preferred_element_type=F32)


def iota(shape, axis):
    return lax.broadcasted_iota(jnp.int32, shape, axis)


def rotary_tables():
    half = HD // 2
    frequency = np.power(np.float32(THETA), -2.0 * np.arange(half, dtype=np.float32) / np.float32(HD)).astype(np.float32)
    angles = ((CACHED + np.arange(SLOT)).astype(np.float32)[:, None] * frequency[None, :]).astype(np.float32)
    cosine, sine = np.cos(angles), np.sin(angles)
    both = np.concatenate([cosine, cosine, -sine, sine], axis=1).astype(np.float32)
    terms, rest = [], both
    for _ in range(3):
        term = rest.astype(jnp.bfloat16)
        terms.append(term)
        rest = rest - term.astype(np.float32)
    table = np.zeros((HD, 3 * 2 * HD), dtype=jnp.bfloat16)
    table[:SLOT] = np.concatenate(terms, axis=1)
    return table


def kernel(
    tokens_hbm, weight_hbm, gain_ref, bias_ref, lengths_ref, dest_ref, query_hbm, old_hbm, new_ref, table_ref,
    out_ref,
    tokens, scaled, weight, query, old,
    pair_out, pair_in, own, from_low, from_high, line_out, final,
    squares, pick, cos_rows, sin_rows, score_old, score_new, outgoing, arrived,
    load_sem, weight_sem, sq_send, sq_recv, pair_send, pair_recv, line_send, low_recv, high_recv, hand_send, hand_recv,
):
    group = lax.axis_index("grp")
    tp = lax.axis_index("tp")
    chip = tp // 2
    core = tp % 2
    partner = tp + 1 - 2 * core

    load_tokens = pltpu.make_async_copy(tokens_hbm, tokens, load_sem.at[0])
    load_tokens.start()

    def head_of(step, whose):
        place = jnp.where(chip < 2, CHIPS - 1 - step, step)
        return place, 2 * place + whose

    def load_weight(step, which):
        whose = (1 - core) if which == 0 else core
        _, head = head_of(step, whose)
        columns = pl.ds(pl.multiple_of(head * WIDTH, WIDTH), WIDTH)
        return pltpu.make_async_copy(weight_hbm.at[:, columns], weight.at[4 * which + step], weight_sem.at[4 * which + step])

    for which in range(2):
        for step in range(CHIPS):
            load_weight(step, which).start()
    load_query = pltpu.make_async_copy(query_hbm, query, load_sem.at[1])
    load_old = pltpu.make_async_copy(old_hbm, old, load_sem.at[2])
    load_query.start()
    load_old.start()

    barrier = pltpu.get_barrier_semaphore()

    def greet_tp(i, carry):
        pl.semaphore_signal(barrier, inc=1, device_id={"tp": (tp + i) % TP}, device_id_type=MESH)
        return carry

    def greet_grp(i, carry):
        pl.semaphore_signal(barrier, inc=1, device_id={"grp": (group + i) % GRP}, device_id_type=MESH)
        return carry

    lax.fori_loop(1, TP, greet_tp, 0)
    lax.fori_loop(1, GRP, greet_grp, 0)

    load_tokens.wait()
    for h in range(2):
        rows = pl.ds(h * HALF, HALF)
        floats = tokens[rows, :].astype(F32)
        scaled[rows, :] = (floats * gain_ref[...]).astype(BF16)
        square = floats * floats
        high = square.astype(BF16)
        low = (square - high.astype(F32)).astype(BF16)
        ones = jnp.ones((8, FEATS), BF16)
        sums = dot(ones, high, NT) + dot(ones, low, NT)
        squares[pl.ds(tp, 1), :, h * HALF:(h + 1) * HALF] = sums[0:1, :].reshape(1, 1, HALF)

    def pair_copy(place):
        return pltpu.make_async_remote_copy(
            src_ref=pair_out.at[place], dst_ref=pair_in.at[place],
            send_sem=pair_send.at[place], recv_sem=pair_recv.at[place],
            device_id={"tp": partner}, device_id_type=MESH,
        )

    def square_copy(i):
        return pltpu.make_async_remote_copy(
            src_ref=squares.at[tp], dst_ref=squares.at[tp],
            send_sem=sq_send.at[i], recv_sem=sq_recv.at[tp],
            device_id={"tp": (tp + i) % TP}, device_id_type=MESH,
        )

    def square_arrival(i):
        source = (tp + i) % TP
        return pltpu.make_async_remote_copy(
            src_ref=squares.at[source], dst_ref=squares.at[source],
            send_sem=sq_send.at[i], recv_sem=sq_recv.at[source],
            device_id={"tp": source}, device_id_type=MESH,
        )

    for step in range(CHIPS):
        place, _ = head_of(step, 0)
        load_weight(step, 0).wait()
        pair_out[pl.ds(place, 1)] = dot(scaled[...], weight[step]).astype(BF16)[None]
        if step == 0:
            pl.semaphore_wait(barrier, TP - 1 + GRP - 1)
        pair_copy(place).start()
    for i in range(1, TP):
        square_copy(i).start()
    for step in range(CHIPS):
        place, _ = head_of(step, 0)
        load_weight(step, 1).wait()
        own[pl.ds(place, 1)] = dot(scaled[...], weight[4 + step])[None]

    def line_copy(direction, place, h):
        rows = pl.ds(h * HALF, HALF)
        landing, sems = (from_low, low_recv) if direction > 0 else (from_high, high_recv)
        return pltpu.make_async_remote_copy(
            src_ref=line_out.at[place, rows], dst_ref=landing.at[place, rows],
            send_sem=line_send.at[place, h], recv_sem=sems.at[place, h],
            device_id={"tp": tp + 2 * direction}, device_id_type=MESH,
        )

    def line_arrival(direction, place, h):
        rows = pl.ds(h * HALF, HALF)
        landing, sems = (from_low, low_recv) if direction > 0 else (from_high, high_recv)
        return pltpu.make_async_remote_copy(
            src_ref=line_out.at[place, rows], dst_ref=landing.at[place, rows],
            send_sem=line_send.at[place, h], recv_sem=sems.at[place, h],
            device_id={"tp": tp - 2 * direction}, device_id_type=MESH,
        )

    def block(place, h):
        rows = pl.ds(h * HALF, HALF)
        return own[place, rows] + pair_in[place, rows].astype(F32)

    def forward(here, direction, place, h):
        rows = pl.ds(h * HALF, HALF)
        first = (here == 0) if direction > 0 else (here == CHIPS - 1)
        value = block(place, h)
        if not first:
            line_arrival(direction, place, h).wait_recv()
            landing = from_low if direction > 0 else from_high
            value = value + landing[place, rows].astype(F32)
        line_out[place, rows] = value.astype(BF16)
        line_copy(direction, place, h).start()

    for here, direction, places in ((0, 1, (3, 2, 1)), (CHIPS - 1, -1, (0, 1, 2))):
        @pl.when(chip == here)
        def _(here=here, direction=direction, places=places):
            for place in places:
                pair_copy(place).wait_recv()
                for h in range(2):
                    forward(here, direction, place, h)

    lengths = lengths_ref[...]
    dests = dest_ref[...]
    mine = iota((GRP, GRP), 0) == group
    own_lengths = jnp.sum(jnp.where(mine, lengths, 0), axis=0, keepdims=True)
    own_dest = jnp.sum(jnp.where(mine, dests, 0), axis=0, keepdims=True)
    before = (iota((GRP, GRP), 0) < iota((GRP, GRP), 1)).astype(F32)
    spread = jnp.broadcast_to(own_lengths.astype(F32), (8, GRP))
    starts = dot(spread, before)[0:1, :].astype(jnp.int32)
    routed = own_dest == iota((GRP, GRP), 0)
    slot_first = jnp.sum(jnp.where(routed, starts, 0), axis=1, keepdims=True)
    slot_length = jnp.sum(jnp.where(routed, own_lengths, 0), axis=1, keepdims=True)
    for part in range(8):
        requests = slice(part * 8, part * 8 + 8)
        offset = iota((8, SLOT, ROWS), 1)
        first = slot_first[requests][:, :, None]
        length = slot_length[requests][:, :, None]
        hit = (iota((8, SLOT, ROWS), 2) == first + offset) & (offset < length)
        pick[part * 128:part * 128 + 128, :] = hit.astype(F32).reshape(128, ROWS).astype(BF16)

    row_index = iota((ROWS, GRP), 0)
    first_row = jnp.max(jnp.where(starts <= row_index, starts, 0), axis=1, keepdims=True)
    at_offset = (iota((ROWS, HD), 1) + first_row == iota((ROWS, HD), 0)).astype(F32).astype(BF16)
    tabled = dot(at_offset, table_ref[...])
    cos_rows[...] = tabled[:, 0:128] + tabled[:, 256:384] + tabled[:, 512:640]
    sin_rows[...] = tabled[:, 128:256] + tabled[:, 384:512] + tabled[:, 640:768]

    toward_me = dests == group
    live = jnp.sum(jnp.where(toward_me, lengths, 0), axis=1, keepdims=True)
    at_source = iota((GRP, SLOTS), 1) // SLOT == iota((GRP, SLOTS), 0)
    live_lanes = jnp.sum(jnp.where(at_source, live, 0), axis=0, keepdims=True)
    live_lanes = (iota((1, SLOTS), 1) % SLOT < live_lanes).astype(F32)

    load_query.wait()
    load_old.wait()
    scale = 1.0 / math.sqrt(HD)
    same = iota((128, 128), 0) // 16 == iota((128, 128), 1) // 16
    same_new = (iota((128, 16), 0) // 16 == iota((128, 16), 1) // 2) & (iota((128, 16), 1) % 2 <= iota((128, 16), 0) % 2)
    for part in range(8):
        rows = slice(part * 128, part * 128 + 128)
        new_rows = slice(part * 16, part * 16 + 16)
        score_old[rows, :] = jnp.where(same, dot(query[rows, :], old[rows, 0:HD], NT) * scale, -1e30)
        score_new[rows, :] = jnp.where(same_new, dot(query[rows, :], new_ref[new_rows, 0:HD], NT) * scale, -1e30)

    schedules = {
        0: [(-1, 0, 0), (-1, 0, 1)],
        1: [(1, 3, 0), (1, 3, 1), (-1, 0, 0), (1, 2, 0), (-1, 0, 1), (1, 2, 1), (-1, 1, 0), (-1, 1, 1), (1, 1, 0), (1, 1, 1)],
        2: [(-1, 0, 0), (-1, 0, 1), (1, 3, 0), (-1, 1, 0), (1, 3, 1), (-1, 1, 1), (1, 2, 0), (1, 2, 1), (-1, 2, 0), (-1, 2, 1)],
        3: [(1, 3, 0), (1, 3, 1)],
    }
    for here in range(CHIPS):
        @pl.when(chip == here)
        def _(here=here):
            have = {0: {3, 2, 1}, 3: {0, 1, 2}}.get(here, set())
            begun = set()
            for direction, place, h in schedules[here]:
                if place not in have:
                    have.add(place)
                    pair_copy(place).wait_recv()
                rows = pl.ds(h * HALF, HALF)
                if place != here:
                    forward(here, direction, place, h)
                    continue
                value = final[rows, :] if h in begun else block(place, h)
                begun.add(h)
                line_arrival(direction, place, h).wait_recv()
                landing = from_low if direction > 0 else from_high
                final[rows, :] = value + landing[place, rows].astype(F32)

    for i in range(1, TP):
        square_arrival(i).wait_recv()
    total = jnp.sum(squares[...].reshape(TP, ROWS), axis=0, keepdims=True)
    inv_rms = lax.rsqrt(total / D + EPSILON)
    inv_rms = jnp.broadcast_to(inv_rms, (HD, ROWS)).T
    keys = final[:, 0:HD] * inv_rms + bias_ref[:, 0:HD]
    values = final[:, HD:WIDTH] * inv_rms + bias_ref[:, HD:WIDTH]
    turned = pltpu.roll(keys, HD // 2, 1)
    keys = (keys * cos_rows[...] + turned * sin_rows[...]).astype(BF16)
    handed = jnp.concatenate([keys, values.astype(BF16)], axis=1)
    outgoing[...] = dot(pick[...], handed).astype(BF16)

    y, x, z = group // 16, (group // 4) % 4, group % 4

    def hand_copy(away, i):
        target = ((y + i // 4) % 4 * 4 + (x + i % 4) % 4) * 4 + (z + away) % 4
        return pltpu.make_async_remote_copy(
            src_ref=outgoing.at[pl.ds(target * SLOT, SLOT)], dst_ref=arrived.at[pl.ds(group * SLOT, SLOT)],
            send_sem=hand_send.at[away * 16 + i], recv_sem=hand_recv.at[away * 16 + i],
            device_id={"grp": target}, device_id_type=MESH,
        )

    def hand_arrival(away, i):
        source = ((y + 4 - i // 4) % 4 * 4 + (x + 4 - i % 4) % 4) * 4 + (z + 4 - away) % 4
        return pltpu.make_async_remote_copy(
            src_ref=outgoing.at[pl.ds(source * SLOT, SLOT)], dst_ref=arrived.at[pl.ds(source * SLOT, SLOT)],
            send_sem=hand_send.at[away * 16 + i], recv_sem=hand_recv.at[away * 16 + i],
            device_id={"grp": source}, device_id_type=MESH,
        )

    def send(away):
        def body(i, carry):
            hand_copy(away, i).start()
            return carry
        return body

    def receive(away):
        def body(i, carry):
            hand_arrival(away, i).wait_recv()
            return carry
        return body

    def sent(away):
        def body(i, carry):
            hand_copy(away, i).wait_send()
            return carry
        return body

    for away in (2, 1, 3, 0):
        lax.fori_loop(0 if away else 1, 16, send(away), 0)
    own_rows = pl.ds(pl.multiple_of(group * SLOT, SLOT), SLOT)
    arrived[own_rows, :] = outgoing[own_rows, :]
    for away in (0, 1, 3, 2):
        lax.fori_loop(0 if away else 1, 16, receive(away), 0)

    for part in range(8):
        rows = slice(part * 128, part * 128 + 128)
        new_rows = slice(part * 16, part * 16 + 16)
        span_live = same & (live_lanes[:, rows] > 0.5)
        cached, fresh = score_old[rows, :], score_new[rows, :]
        span = jnp.where(span_live, dot(query[rows, :], arrived[rows, 0:HD], NT) * scale, -1e30)
        top = jnp.maximum(jnp.max(jnp.maximum(cached, span), axis=1, keepdims=True), jnp.max(fresh, axis=1, keepdims=True))
        cached, span, fresh = jnp.exp(cached - top), jnp.exp(span - top), jnp.exp(fresh - top)
        weight_sum = jnp.sum(cached + span, axis=1, keepdims=True) + jnp.sum(fresh, axis=1, keepdims=True)
        inverse = 1.0 / weight_sum
        result = dot((cached * inverse).astype(BF16), old[rows, HD:WIDTH])
        result = result + dot((span * inverse).astype(BF16), arrived[rows, HD:WIDTH])
        result = result + dot((fresh * inverse).astype(BF16), new_ref[new_rows, HD:WIDTH])
        out_ref[rows, :] = result.astype(BF16)

    for place in range(CHIPS):
        pair_copy(place).wait_send()
        for h in range(2):
            @pl.when(chip != place)
            def _(place=place, h=h):
                rows = pl.ds(h * HALF, HALF)
                pltpu.make_async_remote_copy(
                    src_ref=line_out.at[place, rows], dst_ref=from_low.at[place, rows],
                    send_sem=line_send.at[place, h], recv_sem=low_recv.at[place, h],
                    device_id={"tp": partner}, device_id_type=MESH,
                ).wait_send()
    for i in range(1, TP):
        square_copy(i).wait_send()
    for away in (0, 1, 3, 2):
        lax.fori_loop(0 if away else 1, 16, sent(away), 0)


def shards(tokens, gain, kv_weight, kv_bias, lengths, dest, queries, old_cache, new_kv):
    query_rows = queries.reshape(GRP, STEPS, QPK, HD).transpose(0, 2, 1, 3).reshape(SLOTS, HD)
    any_space = pl.BlockSpec(memory_space=pl.ANY)
    vmem = pl.BlockSpec(memory_space=pltpu.VMEM)
    dma = pltpu.SemaphoreType.DMA
    out = pl.pallas_call(
        kernel,
        out_shape=jax.ShapeDtypeStruct((SLOTS, HD), BF16),
        in_specs=[any_space, any_space, vmem, vmem, vmem, vmem, any_space, any_space, vmem, vmem],
        out_specs=vmem,
        scratch_shapes=[
            pltpu.VMEM((ROWS, FEATS), BF16),
            pltpu.VMEM((ROWS, FEATS), BF16),
            pltpu.VMEM((TP, FEATS, WIDTH), BF16),
            pltpu.VMEM((SLOTS, HD), BF16),
            pltpu.VMEM((SLOTS, WIDTH), BF16),
            pltpu.VMEM((CHIPS, ROWS, WIDTH), BF16),
            pltpu.VMEM((CHIPS, ROWS, WIDTH), BF16),
            pltpu.VMEM((CHIPS, ROWS, WIDTH), F32),
            pltpu.VMEM((CHIPS, ROWS, WIDTH), BF16),
            pltpu.VMEM((CHIPS, ROWS, WIDTH), BF16),
            pltpu.VMEM((CHIPS, ROWS, WIDTH), BF16),
            pltpu.VMEM((ROWS, WIDTH), F32),
            pltpu.VMEM((TP, 1, ROWS), F32),
            pltpu.VMEM((SLOTS, ROWS), BF16),
            pltpu.VMEM((ROWS, HD), F32),
            pltpu.VMEM((ROWS, HD), F32),
            pltpu.VMEM((SLOTS, 128), F32),
            pltpu.VMEM((SLOTS, 16), F32),
            pltpu.VMEM((SLOTS, WIDTH), BF16),
            pltpu.VMEM((SLOTS, WIDTH), BF16),
            dma((3,)),
            dma((TP,)),
            dma((TP,)),
            dma((TP,)),
            dma((CHIPS,)),
            dma((CHIPS,)),
            dma((CHIPS, 2)),
            dma((CHIPS, 2)),
            dma((CHIPS, 2)),
            dma((GRP,)),
            dma((GRP,)),
        ],
        compiler_params=pltpu.CompilerParams(
            collective_id=0, has_side_effects=True, vmem_limit_bytes=48 * 1024 * 1024
        ),
        cost_estimate=pl.CostEstimate(flops=2_500_000_000, bytes_accessed=6_000_000, transcendentals=300_000),
    )(
        tokens, kv_weight, gain.reshape(1, FEATS), kv_bias.reshape(1, WIDTH), lengths, dest,
        query_rows, old_cache.reshape(SLOTS, WIDTH), new_kv.reshape(GRP * STEPS, WIDTH), jnp.asarray(rotary_tables()),
    )
    return out.reshape(GRP, QPK, STEPS, HD).transpose(0, 2, 1, 3).reshape(1, GRP, STEPS, QPK * HD)


def solution(mesh):
    return jax.shard_map(
        shards,
        mesh=mesh,
        in_specs=(
            P("grp", "tp"),
            P("tp"),
            P("tp", None),
            P("tp"),
            P(),
            P(),
            P("grp", None, None, "tp"),
            P("grp", None, None, "tp"),
            P("grp", None, None, "tp"),
        ),
        out_specs=P("grp", None, None, "tp"),
        check_vma=False,
    )
```

```python
import functools
import math

import jax
import jax.numpy as jnp
import numpy as np
from jax import lax
from jax.experimental import pallas as pl
from jax.experimental.pallas import tpu as pltpu
from jax.sharding import PartitionSpec as P

D = 6144
HD = 128
SLOT = 16
CACHED = 16
STEPS = 2
KVW = 2048
QPK = 8
EPSILON = 1e-06
THETA = 1000000.0

ROWS = 512
FEATS = 768
GRP = 64
TP = 8
CHIPS = 4
WIDTH = 256
HALF = ROWS // 2
SLOTS = GRP * SLOT
MESH = pl.DeviceIdType.MESH
F32 = jnp.float32
BF16 = jnp.bfloat16
NT = (((1,), (1,)), ((), ()))
NN = (((1,), (0,)), ((), ()))


def dot(a, b, dims=NN):
    return lax.dot_general(a, b, dims, preferred_element_type=F32)


def iota(shape, axis):
    return lax.broadcasted_iota(jnp.int32, shape, axis)


def rotary_tables():
    half = HD // 2
    frequency = np.power(np.float32(THETA), -2.0 * np.arange(half, dtype=np.float32) / np.float32(HD)).astype(np.float32)
    angles = ((CACHED + np.arange(SLOT)).astype(np.float32)[:, None] * frequency[None, :]).astype(np.float32)
    cosine, sine = np.cos(angles), np.sin(angles)
    return np.concatenate([cosine, cosine, -sine, sine], axis=1).astype(np.float32)


def kernel(
    tokens_hbm, weight_hbm, gain_hbm, bias_hbm, lengths_hbm, dest_hbm, query_hbm, old_hbm, new_hbm, table_hbm,
    out_ref,
    tokens, scaled, weight, gain_ref, bias_ref, lengths_ref, dest_ref, query, old, new_ref, new_values, table_ref,
    pair_out, pair_in, own, from_low, from_high, line_out, final,
    squares, pick, cos_rows, sin_rows, score_old, score_new, outgoing, arrived,
    load_sem, weight_sem, sq_send, sq_recv, pair_send, pair_recv, line_send, low_recv, high_recv, hand_send, hand_recv,
):
    group = lax.axis_index("grp")
    tp = lax.axis_index("tp")
    chip = tp // 2
    core = tp % 2
    partner = tp + 1 - 2 * core

    load_gain = pltpu.make_async_copy(gain_hbm, gain_ref, load_sem.at[0])
    load_tokens = pltpu.make_async_copy(tokens_hbm, tokens, load_sem.at[1])
    load_gain.start()
    load_tokens.start()

    def head_of(step, whose):
        place = jnp.where(chip < 2, CHIPS - 1 - step, step)
        return place, 2 * place + whose

    def load_weight(step, which):
        whose = (1 - core) if which == 0 else core
        _, head = head_of(step, whose)
        columns = pl.ds(pl.multiple_of(head * WIDTH, WIDTH), WIDTH)
        return pltpu.make_async_copy(weight_hbm.at[:, columns], weight.at[4 * which + step], weight_sem.at[4 * which + step])

    for which in range(2):
        for step in range(CHIPS):
            load_weight(step, which).start()
    later_loads = [
        pltpu.make_async_copy(source, target, load_sem.at[2 + i])
        for i, (source, target) in enumerate((
            (lengths_hbm, lengths_ref), (dest_hbm, dest_ref), (table_hbm, table_ref), (bias_hbm, bias_ref),
            (query_hbm, query), (old_hbm, old), (new_hbm, new_ref),
        ))
    ]
    for load in later_loads:
        load.start()

    barrier = pltpu.get_barrier_semaphore()

    def greet_tp(i, carry):
        pl.semaphore_signal(barrier, inc=1, device_id={"tp": (tp + i) % TP}, device_id_type=MESH)
        return carry

    def greet_grp(i, carry):
        pl.semaphore_signal(barrier, inc=1, device_id={"grp": (group + i) % GRP}, device_id_type=MESH)
        return carry

    lax.fori_loop(1, TP, greet_tp, 0)
    lax.fori_loop(1, GRP, greet_grp, 0)

    load_gain.wait()
    load_tokens.wait()
    for h in range(2):
        rows = pl.ds(h * HALF, HALF)
        floats = tokens[rows, :].astype(F32)
        scaled[rows, :] = (floats * gain_ref[...][None, :]).astype(BF16)
        square = floats * floats
        high = square.astype(BF16)
        low = (square - high.astype(F32)).astype(BF16)
        ones = jnp.ones((8, FEATS), BF16)
        sums = dot(ones, high, NT) + dot(ones, low, NT)
        squares[pl.ds(tp, 1), :, h * HALF:(h + 1) * HALF] = sums[0:1, :].reshape(1, 1, HALF)

    def pair_copy(place):
        return pltpu.make_async_remote_copy(
            src_ref=pair_out.at[place], dst_ref=pair_in.at[place],
            send_sem=pair_send.at[place], recv_sem=pair_recv.at[place],
            device_id={"tp": partner}, device_id_type=MESH,
        )

    def square_copy(i):
        return pltpu.make_async_remote_copy(
            src_ref=squares.at[tp], dst_ref=squares.at[tp],
            send_sem=sq_send.at[i], recv_sem=sq_recv.at[tp],
            device_id={"tp": (tp + i) % TP}, device_id_type=MESH,
        )

    def square_arrival(i):
        source = (tp + i) % TP
        return pltpu.make_async_remote_copy(
            src_ref=squares.at[source], dst_ref=squares.at[source],
            send_sem=sq_send.at[i], recv_sem=sq_recv.at[source],
            device_id={"tp": source}, device_id_type=MESH,
        )

    for step in range(CHIPS):
        place, _ = head_of(step, 0)
        load_weight(step, 0).wait()
        pair_out[pl.ds(place, 1)] = dot(scaled[...], weight[step]).astype(BF16)[None]
        if step == 0:
            pl.semaphore_wait(barrier, TP - 1 + GRP - 1)
        pair_copy(place).start()
    for i in range(1, TP):
        square_copy(i).start()
    for step in range(CHIPS):
        place, _ = head_of(step, 0)
        load_weight(step, 1).wait()
        own[pl.ds(place, 1)] = dot(scaled[...], weight[4 + step])[None]

    def line_copy(direction, place, h):
        rows = pl.ds(h * HALF, HALF)
        landing, sems = (from_low, low_recv) if direction > 0 else (from_high, high_recv)
        return pltpu.make_async_remote_copy(
            src_ref=line_out.at[place, rows], dst_ref=landing.at[place, rows],
            send_sem=line_send.at[place, h], recv_sem=sems.at[place, h],
            device_id={"tp": tp + 2 * direction}, device_id_type=MESH,
        )

    def line_arrival(direction, place, h):
        rows = pl.ds(h * HALF, HALF)
        landing, sems = (from_low, low_recv) if direction > 0 else (from_high, high_recv)
        return pltpu.make_async_remote_copy(
            src_ref=line_out.at[place, rows], dst_ref=landing.at[place, rows],
            send_sem=line_send.at[place, h], recv_sem=sems.at[place, h],
            device_id={"tp": tp - 2 * direction}, device_id_type=MESH,
        )

    def block(place, h):
        rows = pl.ds(h * HALF, HALF)
        return own[place, rows] + pair_in[place, rows].astype(F32)

    def forward(here, direction, place, h):
        rows = pl.ds(h * HALF, HALF)
        first = (here == 0) if direction > 0 else (here == CHIPS - 1)
        value = block(place, h)
        if not first:
            line_arrival(direction, place, h).wait_recv()
            landing = from_low if direction > 0 else from_high
            value = value + landing[place, rows].astype(F32)
        line_out[place, rows] = value.astype(BF16)
        line_copy(direction, place, h).start()

    for here, direction, places in ((0, 1, (3, 2, 1)), (CHIPS - 1, -1, (0, 1, 2))):
        @pl.when(chip == here)
        def _(here=here, direction=direction, places=places):
            for place in places:
                pair_copy(place).wait_recv()
                for h in range(2):
                    forward(here, direction, place, h)

    for load in later_loads:
        load.wait()
    lengths = lengths_ref[...]
    dests = dest_ref[...]
    mine = iota((GRP, GRP), 0) == group
    own_lengths = jnp.sum(jnp.where(mine, lengths, 0), axis=0, keepdims=True)
    own_dest = jnp.sum(jnp.where(mine, dests, 0), axis=0, keepdims=True)
    before = (iota((GRP, GRP), 0) < iota((GRP, GRP), 1)).astype(F32)
    spread = jnp.broadcast_to(own_lengths.astype(F32), (8, GRP))
    starts = dot(spread, before)[0:1, :].astype(jnp.int32)
    routed = own_dest == iota((GRP, GRP), 0)
    slot_first = jnp.sum(jnp.where(routed, starts, 0), axis=1, keepdims=True)
    slot_length = jnp.sum(jnp.where(routed, own_lengths, 0), axis=1, keepdims=True)
    for part in range(8):
        requests = slice(part * 8, part * 8 + 8)
        offset = iota((8, SLOT, ROWS), 1)
        first = slot_first[requests][:, :, None]
        length = slot_length[requests][:, :, None]
        hit = (iota((8, SLOT, ROWS), 2) == first + offset) & (offset < length)
        pick[part * 128:part * 128 + 128, :] = hit.astype(F32).reshape(128, ROWS).astype(BF16)

    row_index = iota((ROWS, GRP), 0)
    first_row = jnp.max(jnp.where(starts <= row_index, starts, 0), axis=1, keepdims=True)
    at_offset = (iota((ROWS, SLOT), 1) + first_row == iota((ROWS, SLOT), 0)).astype(F32).astype(BF16)
    rest = table_ref[...]
    tabled = jnp.zeros((ROWS, 2 * HD), F32)
    for _ in range(3):
        term = rest.astype(BF16)
        rest = rest - term.astype(F32)
        tabled = tabled + dot(at_offset, term)
    cos_rows[...] = tabled[:, 0:HD]
    sin_rows[...] = tabled[:, HD:2 * HD]

    toward_me = dests == group
    live = jnp.sum(jnp.where(toward_me, lengths, 0), axis=1, keepdims=True)
    at_source = iota((GRP, SLOTS), 1) // SLOT == iota((GRP, SLOTS), 0)
    live_lanes = jnp.sum(jnp.where(at_source, live, 0), axis=0, keepdims=True)
    live_lanes = (iota((1, SLOTS), 1) % SLOT < live_lanes).astype(F32)

    new_values[...] = pltpu.roll(new_ref[...].astype(F32), 4 * GRP - 2, 0).astype(BF16)
    scale = 1.0 / math.sqrt(HD)
    same = iota((128, 128), 0) // 16 == iota((128, 128), 1) // 16
    same_new = (iota((128, 32), 0) // 16 == iota((128, 32), 1) // 4) & (iota((128, 32), 1) % 4 <= iota((128, 32), 0) % 2)
    for part in range(8):
        rows = slice(part * 128, part * 128 + 128)
        new_rows = slice(part * 32, part * 32 + 32)
        score_old[rows, :] = jnp.where(same, dot(query[rows, :], old[rows, 0:HD], NT) * scale, -1e30)
        score_new[rows, :] = jnp.where(same_new, dot(query[rows, :], new_ref[new_rows, :], NT) * scale, -1e30)

    schedules = {
        0: [(-1, 0, 0), (-1, 0, 1)],
        1: [(1, 3, 0), (1, 3, 1), (-1, 0, 0), (1, 2, 0), (-1, 0, 1), (1, 2, 1), (-1, 1, 0), (-1, 1, 1), (1, 1, 0), (1, 1, 1)],
        2: [(-1, 0, 0), (-1, 0, 1), (1, 3, 0), (-1, 1, 0), (1, 3, 1), (-1, 1, 1), (1, 2, 0), (1, 2, 1), (-1, 2, 0), (-1, 2, 1)],
        3: [(1, 3, 0), (1, 3, 1)],
    }
    for here in range(CHIPS):
        @pl.when(chip == here)
        def _(here=here):
            have = {0: {3, 2, 1}, 3: {0, 1, 2}}.get(here, set())
            begun = set()
            for direction, place, h in schedules[here]:
                if place not in have:
                    have.add(place)
                    pair_copy(place).wait_recv()
                rows = pl.ds(h * HALF, HALF)
                if place != here:
                    forward(here, direction, place, h)
                    continue
                value = final[rows, :] if h in begun else block(place, h)
                begun.add(h)
                line_arrival(direction, place, h).wait_recv()
                landing = from_low if direction > 0 else from_high
                final[rows, :] = value + landing[place, rows].astype(F32)

    for i in range(1, TP):
        square_arrival(i).wait_recv()
    total = jnp.sum(squares[...].reshape(TP, ROWS), axis=0, keepdims=True)
    inv_rms = lax.rsqrt(total / D + EPSILON)
    inv_rms = jnp.broadcast_to(inv_rms, (HD, ROWS)).T
    keys = final[:, 0:HD] * inv_rms + bias_ref[0:HD][None, :]
    values = final[:, HD:WIDTH] * inv_rms + bias_ref[HD:WIDTH][None, :]
    turned = pltpu.roll(keys, HD // 2, 1)
    keys = (keys * cos_rows[...] + turned * sin_rows[...]).astype(BF16)
    handed = jnp.concatenate([keys, values.astype(BF16)], axis=1)
    outgoing[...] = dot(pick[...], handed).astype(BF16)

    y, x, z = group // 16, (group // 4) % 4, group % 4

    def hand_copy(away, i):
        target = ((y + i // 4) % 4 * 4 + (x + i % 4) % 4) * 4 + (z + away) % 4
        return pltpu.make_async_remote_copy(
            src_ref=outgoing.at[pl.ds(target * SLOT, SLOT)], dst_ref=arrived.at[pl.ds(group * SLOT, SLOT)],
            send_sem=hand_send.at[away * 16 + i], recv_sem=hand_recv.at[away * 16 + i],
            device_id={"grp": target}, device_id_type=MESH,
        )

    def hand_arrival(away, i):
        source = ((y + 4 - i // 4) % 4 * 4 + (x + 4 - i % 4) % 4) * 4 + (z + 4 - away) % 4
        return pltpu.make_async_remote_copy(
            src_ref=outgoing.at[pl.ds(source * SLOT, SLOT)], dst_ref=arrived.at[pl.ds(source * SLOT, SLOT)],
            send_sem=hand_send.at[away * 16 + i], recv_sem=hand_recv.at[away * 16 + i],
            device_id={"grp": source}, device_id_type=MESH,
        )

    def send(away):
        def body(i, carry):
            hand_copy(away, i).start()
            return carry
        return body

    def receive(away):
        def body(i, carry):
            hand_arrival(away, i).wait_recv()
            return carry
        return body

    def sent(away):
        def body(i, carry):
            hand_copy(away, i).wait_send()
            return carry
        return body

    for away in (2, 1, 3, 0):
        lax.fori_loop(0 if away else 1, 16, send(away), 0)
    own_rows = pl.ds(pl.multiple_of(group * SLOT, SLOT), SLOT)
    arrived[own_rows, :] = outgoing[own_rows, :]
    for away in (0, 1, 3, 2):
        lax.fori_loop(0 if away else 1, 16, receive(away), 0)

    for part in range(8):
        rows = slice(part * 128, part * 128 + 128)
        new_rows = slice(part * 32, part * 32 + 32)
        span_live = same & (live_lanes[:, rows] > 0.5)
        cached, fresh = score_old[rows, :], score_new[rows, :]
        span = jnp.where(span_live, dot(query[rows, :], arrived[rows, 0:HD], NT) * scale, -1e30)
        top = jnp.maximum(jnp.max(jnp.maximum(cached, span), axis=1, keepdims=True), jnp.max(fresh, axis=1, keepdims=True))
        cached, span, fresh = jnp.exp(cached - top), jnp.exp(span - top), jnp.exp(fresh - top)
        weight_sum = jnp.sum(cached + span, axis=1, keepdims=True) + jnp.sum(fresh, axis=1, keepdims=True)
        inverse = 1.0 / weight_sum
        result = dot((cached * inverse).astype(BF16), old[rows, HD:WIDTH])
        result = result + dot((span * inverse).astype(BF16), arrived[rows, HD:WIDTH])
        result = result + dot((fresh * inverse).astype(BF16), new_values[new_rows, :])
        out_ref[rows, :] = result.astype(BF16)

    for place in range(CHIPS):
        pair_copy(place).wait_send()
        for h in range(2):
            @pl.when(chip != place)
            def _(place=place, h=h):
                rows = pl.ds(h * HALF, HALF)
                pltpu.make_async_remote_copy(
                    src_ref=line_out.at[place, rows], dst_ref=from_low.at[place, rows],
                    send_sem=line_send.at[place, h], recv_sem=low_recv.at[place, h],
                    device_id={"tp": partner}, device_id_type=MESH,
                ).wait_send()
    for i in range(1, TP):
        square_copy(i).wait_send()
    for away in (0, 1, 3, 2):
        lax.fori_loop(0 if away else 1, 16, sent(away), 0)


def shards(tokens, gain, kv_weight, kv_bias, lengths, dest, queries, old_cache, new_kv):
    query_rows = queries.reshape(GRP, STEPS, QPK, HD).transpose(0, 2, 1, 3).reshape(SLOTS, HD)
    new_rows = new_kv.reshape(GRP, STEPS, 2, HD).transpose(0, 2, 1, 3).reshape(4 * GRP, HD)
    any_space = pl.BlockSpec(memory_space=pl.ANY)
    vmem = pl.BlockSpec(memory_space=pltpu.VMEM)
    dma = pltpu.SemaphoreType.DMA
    out = pl.pallas_call(
        kernel,
        out_shape=jax.ShapeDtypeStruct((SLOTS, HD), BF16),
        in_specs=[any_space] * 10,
        out_specs=vmem,
        scratch_shapes=[
            pltpu.VMEM((ROWS, FEATS), BF16),
            pltpu.VMEM((ROWS, FEATS), BF16),
            pltpu.VMEM((TP, FEATS, WIDTH), BF16),
            pltpu.VMEM((FEATS,), F32),
            pltpu.VMEM((WIDTH,), F32),
            pltpu.VMEM((GRP, GRP), jnp.int32),
            pltpu.VMEM((GRP, GRP), jnp.int32),
            pltpu.VMEM((SLOTS, HD), BF16),
            pltpu.VMEM((SLOTS, WIDTH), BF16),
            pltpu.VMEM((4 * GRP, HD), BF16),
            pltpu.VMEM((4 * GRP, HD), BF16),
            pltpu.VMEM((SLOT, 2 * HD), F32),
            pltpu.VMEM((CHIPS, ROWS, WIDTH), BF16),
            pltpu.VMEM((CHIPS, ROWS, WIDTH), BF16),
            pltpu.VMEM((CHIPS, ROWS, WIDTH), F32),
            pltpu.VMEM((CHIPS, ROWS, WIDTH), BF16),
            pltpu.VMEM((CHIPS, ROWS, WIDTH), BF16),
            pltpu.VMEM((CHIPS, ROWS, WIDTH), BF16),
            pltpu.VMEM((ROWS, WIDTH), F32),
            pltpu.VMEM((TP, 1, ROWS), F32),
            pltpu.VMEM((SLOTS, ROWS), BF16),
            pltpu.VMEM((ROWS, HD), F32),
            pltpu.VMEM((ROWS, HD), F32),
            pltpu.VMEM((SLOTS, 128), F32),
            pltpu.VMEM((SLOTS, 32), F32),
            pltpu.VMEM((SLOTS, WIDTH), BF16),
            pltpu.VMEM((SLOTS, WIDTH), BF16),
            dma((9,)),
            dma((TP,)),
            dma((TP,)),
            dma((TP,)),
            dma((CHIPS,)),
            dma((CHIPS,)),
            dma((CHIPS, 2)),
            dma((CHIPS, 2)),
            dma((CHIPS, 2)),
            dma((GRP,)),
            dma((GRP,)),
        ],
        compiler_params=pltpu.CompilerParams(
            collective_id=0, has_side_effects=True, vmem_limit_bytes=60 * 1024 * 1024
        ),
        cost_estimate=pl.CostEstimate(flops=2_500_000_000, bytes_accessed=6_000_000, transcendentals=300_000),
    )(
        tokens, kv_weight, gain, kv_bias, lengths, dest,
        query_rows, old_cache.reshape(SLOTS, WIDTH), new_rows, jnp.asarray(rotary_tables()),
    )
    return out.reshape(GRP, QPK, STEPS, HD).transpose(0, 2, 1, 3).reshape(1, GRP, STEPS, QPK * HD)


def solution(mesh):
    return jax.shard_map(
        shards,
        mesh=mesh,
        in_specs=(
            P("grp", "tp"),
            P("tp"),
            P("tp", None),
            P("tp"),
            P(),
            P(),
            P("grp", None, None, "tp"),
            P("grp", None, None, "tp"),
            P("grp", None, None, "tp"),
        ),
        out_specs=P("grp", None, None, "tp"),
        check_vma=False,
    )
```

```python
import functools
import math

import jax
import jax.numpy as jnp
import numpy as np
from jax import lax
from jax.experimental import pallas as pl
from jax.experimental.pallas import tpu as pltpu
from jax.sharding import PartitionSpec as P

D = 6144
HD = 128
SLOT = 16
CACHED = 16
STEPS = 2
KVW = 2048
QPK = 8
EPSILON = 1e-06
THETA = 1000000.0

ROWS = 512
FEATS = 768
GRP = 64
TP = 8
CHIPS = 4
WIDTH = 256
HALF = ROWS // 2
SLOTS = GRP * SLOT
LAYERS = 4
PLANE = GRP // LAYERS
LANES = PLANE * SLOT
LEADER = 7
MESH = pl.DeviceIdType.MESH
F32 = jnp.float32
BF16 = jnp.bfloat16
NT = (((1,), (1,)), ((), ()))
NN = (((1,), (0,)), ((), ()))


def dot(a, b, dims=NN):
    return lax.dot_general(a, b, dims, preferred_element_type=F32)


def iota(shape, axis):
    return lax.broadcasted_iota(jnp.int32, shape, axis)


def rotary_tables():
    half = HD // 2
    frequency = np.power(np.float32(THETA), -2.0 * np.arange(half, dtype=np.float32) / np.float32(HD)).astype(np.float32)
    angles = ((CACHED + np.arange(SLOT)).astype(np.float32)[:, None] * frequency[None, :]).astype(np.float32)
    cosine, sine = np.cos(angles), np.sin(angles)
    return np.concatenate([cosine, cosine, -sine, sine], axis=1).astype(np.float32)


def kernel(
    tokens_hbm, weight_hbm, gain_hbm, bias_hbm, lengths_hbm, dest_hbm, query_hbm, old_hbm, new_hbm, table_hbm,
    out_ref,
    tokens, scaled, weight, gain_ref, bias_ref, lengths_ref, dest_ref, query, old, new_ref, new_keys, new_values, table_ref,
    pair_out, pair_in, own, landing, line_out, final,
    squares, pick, cos_rows, sin_rows, inverse_rms, live, score_old, score_new, outgoing, arrived,
    joined, all_in,
    load_sem, weight_sem, sq_send, sq_recv, pair_send, pair_recv, line_send, line_recv, hand_send, hand_recv,
):
    group = lax.axis_index("grp")
    tp = lax.axis_index("tp")
    chip = tp // 2
    core = tp % 2
    partner = tp + 1 - 2 * core
    plane, layer = group // LAYERS, group % LAYERS

    load_gain = pltpu.make_async_copy(gain_hbm, gain_ref, load_sem.at[0])
    load_tokens = pltpu.make_async_copy(tokens_hbm, tokens, load_sem.at[1])
    load_gain.start()
    load_tokens.start()

    def head_of(step, whose):
        place = jnp.where(chip < 2, CHIPS - 1 - step, step)
        return place, 2 * place + whose

    def load_weight(step, which):
        whose = (1 - core) if which == 0 else core
        _, head = head_of(step, whose)
        columns = pl.ds(pl.multiple_of(head * WIDTH, WIDTH), WIDTH)
        return pltpu.make_async_copy(weight_hbm.at[:, columns], weight.at[4 * which + step], weight_sem.at[4 * which + step])

    for step in range(CHIPS):
        for which in range(2):
            load_weight(step, which).start()
    later_loads = [
        (lengths_hbm, lengths_ref), (dest_hbm, dest_ref), (table_hbm, table_ref), (bias_hbm, bias_ref), (new_hbm, new_ref),
    ]
    for z in range(LAYERS):
        later_loads.append((query_hbm.at[:, z], query.at[z]))
        later_loads.append((old_hbm.at[:, z], old.at[z]))
    later_loads = [
        pltpu.make_async_copy(source, target, load_sem.at[2 + i]) for i, (source, target) in enumerate(later_loads)
    ]
    for load in later_loads:
        load.start()

    barrier = pltpu.get_barrier_semaphore()

    def greet_tp(i, carry):
        peer = (tp + i) % TP

        @pl.when(peer != LEADER)
        def _():
            pl.semaphore_signal(barrier, inc=1, device_id={"tp": peer}, device_id_type=MESH)

        return carry

    def greet_leaders(i, carry):
        pl.semaphore_signal(barrier, inc=1, device_id={"grp": (group + i) % GRP}, device_id_type=MESH)
        return carry

    def tell_group(i, carry):
        pl.semaphore_signal(all_in, inc=1, device_id={"tp": (tp + i) % TP}, device_id_type=MESH)
        return carry

    lax.fori_loop(1, TP, greet_tp, 0)

    @pl.when(tp != LEADER)
    def _():
        pl.semaphore_wait(barrier, TP - 1)
        pl.semaphore_signal(joined, inc=1, device_id={"tp": LEADER}, device_id_type=MESH)

    load_gain.wait()
    load_tokens.wait()
    for h in range(2):
        rows = pl.ds(h * HALF, HALF)
        scaled[rows, :] = (tokens[rows, :].astype(F32) * gain_ref[...][None, :]).astype(BF16)

    def pair_copy(place):
        return pltpu.make_async_remote_copy(
            src_ref=pair_out.at[place], dst_ref=pair_in.at[place],
            send_sem=pair_send.at[place], recv_sem=pair_recv.at[place],
            device_id={"tp": partner}, device_id_type=MESH,
        )

    def line_copy(way, place, h, to):
        rows = pl.ds(h * HALF, HALF)
        return pltpu.make_async_remote_copy(
            src_ref=line_out.at[place, rows], dst_ref=landing.at[way, place, rows],
            send_sem=line_send.at[place, h], recv_sem=line_recv.at[way, place, h],
            device_id={"tp": to}, device_id_type=MESH,
        )

    def block(place, h):
        rows = pl.ds(h * HALF, HALF)
        return own[place, rows] + pair_in[place, rows].astype(F32)

    def multiply_pair(step):
        place, _ = head_of(step, 0)
        load_weight(step, 0).wait()
        pair_out[pl.ds(place, 1)] = dot(scaled[...], weight[step]).astype(BF16)[None]
        if step == 0:
            @pl.when(tp == LEADER)
            def _():
                pl.semaphore_wait(joined, TP - 1)
                lax.fori_loop(1, GRP, greet_leaders, 0)
        pair_copy(place).start()

    def multiply_own(step):
        place, _ = head_of(step, 0)
        load_weight(step, 1).wait()
        own[pl.ds(place, 1)] = dot(scaled[...], weight[4 + step])[None]

    def first_sends(step):
        place, _ = head_of(step, 0)
        way = chip // (CHIPS - 1)

        @pl.when(chip % (CHIPS - 1) == 0)
        def _():
            pair_copy(place).wait_recv()
            for h in range(2):
                rows = pl.ds(h * HALF, HALF)
                line_out[place, rows] = block(place, h).astype(BF16)
                line_copy(way, place, h, tp + 2 - 4 * way).start()

    multiply_pair(0)
    multiply_own(0)
    for step in range(1, CHIPS):
        multiply_pair(step)
        first_sends(step - 1)
        multiply_own(step)

    def square_copy(i):
        return pltpu.make_async_remote_copy(
            src_ref=squares.at[tp], dst_ref=squares.at[tp],
            send_sem=sq_send.at[i], recv_sem=sq_recv.at[tp],
            device_id={"tp": (tp + i) % TP}, device_id_type=MESH,
        )

    def square_arrival(i):
        source = (tp + i) % TP
        return pltpu.make_async_remote_copy(
            src_ref=squares.at[source], dst_ref=squares.at[source],
            send_sem=sq_send.at[i], recv_sem=sq_recv.at[source],
            device_id={"tp": source}, device_id_type=MESH,
        )

    for h in range(2):
        floats = tokens[pl.ds(h * HALF, HALF), :].astype(F32)
        square = floats * floats
        high = square.astype(BF16)
        low = (square - high.astype(F32)).astype(BF16)
        ones = jnp.ones((8, FEATS), BF16)
        sums = dot(ones, high, NT) + dot(ones, low, NT)
        squares[pl.ds(tp, 1), :, h * HALF:(h + 1) * HALF] = sums[0:1, :].reshape(1, 1, HALF)
    for i in range(1, TP):
        square_copy(i).start()

    for load in later_loads:
        load.wait()
    lengths = lengths_ref[...]
    dests = dest_ref[...]
    mine = iota((GRP, GRP), 0) == group
    own_lengths = jnp.sum(jnp.where(mine, lengths, 0), axis=0, keepdims=True)
    own_dest = jnp.sum(jnp.where(mine, dests, 0), axis=0, keepdims=True)
    before = (iota((GRP, GRP), 0) < iota((GRP, GRP), 1)).astype(F32)
    spread = jnp.broadcast_to(own_lengths.astype(F32), (8, GRP))
    starts = dot(spread, before)[0:1, :].astype(jnp.int32)
    by_layer = iota((GRP, GRP), 0) % PLANE * LAYERS + iota((GRP, GRP), 0) // PLANE
    routed = own_dest == by_layer
    slot_first = jnp.sum(jnp.where(routed, starts, 0), axis=1, keepdims=True)
    slot_length = jnp.sum(jnp.where(routed, own_lengths, 0), axis=1, keepdims=True)
    for part in range(8):
        requests = slice(part * 8, part * 8 + 8)
        offset = iota((8, SLOT, ROWS), 1)
        first = slot_first[requests][:, :, None]
        length = slot_length[requests][:, :, None]
        hit = (iota((8, SLOT, ROWS), 2) == first + offset) & (offset < length)
        pick[part // 2, part % 2 * 128:part % 2 * 128 + 128, :] = hit.astype(F32).reshape(128, ROWS).astype(BF16)

    row_index = iota((ROWS, GRP), 0)
    first_row = jnp.max(jnp.where(starts <= row_index, starts, 0), axis=1, keepdims=True)
    at_offset = (iota((ROWS, SLOT), 1) + first_row == iota((ROWS, SLOT), 0)).astype(F32).astype(BF16)
    rest = table_ref[...]
    tabled = jnp.zeros((ROWS, 2 * HD), F32)
    for _ in range(3):
        term = rest.astype(BF16)
        rest = rest - term.astype(F32)
        tabled = tabled + dot(at_offset, term)
    cos_rows[...] = tabled[:, 0:HD]
    sin_rows[...] = tabled[:, HD:2 * HD]

    live_rows = jnp.sum(jnp.where(dests == group, lengths, 0), axis=1, keepdims=True)
    for z in range(LAYERS):
        at_source = iota((GRP, LANES), 1) // SLOT * LAYERS + z == iota((GRP, LANES), 0)
        live_lanes = jnp.sum(jnp.where(at_source, live_rows, 0), axis=0, keepdims=True)
        live[z] = (iota((1, LANES), 1) % SLOT < live_lanes).astype(F32)

    sorted_row = iota((4 * GRP, 4 * GRP), 0)
    natural = (sorted_row // 4 % PLANE * LAYERS + sorted_row // (4 * PLANE)) * 4 + sorted_row % 4
    column = iota((4 * GRP, 4 * GRP), 1)
    new_keys[...] = dot((column == natural).astype(F32).astype(BF16), new_ref[...]).astype(BF16)
    shifted = (column == natural + 2) & (sorted_row % 4 < 2)
    new_values[...] = dot(shifted.astype(F32).astype(BF16), new_ref[...]).astype(BF16)

    scale = 1.0 / math.sqrt(HD)
    same = iota((128, 128), 0) // 16 == iota((128, 128), 1) // 16
    same_new = (iota((128, 32), 0) // 16 == iota((128, 32), 1) // 4) & (iota((128, 32), 1) % 4 <= iota((128, 32), 0) % 2)
    for z in range(LAYERS):
        for half in range(2):
            eight = slice(half * 8, half * 8 + 8)
            asked = query[z, eight].reshape(128, HD)
            cached_keys = old[z, eight, :, 0:HD].reshape(128, HD)
            fresh_keys = new_keys[z * 64 + half * 32:z * 64 + half * 32 + 32, :]
            score_old[2 * z + half] = jnp.where(same, dot(asked, cached_keys, NT) * scale, -1e30)
            score_new[2 * z + half] = jnp.where(same_new, dot(asked, fresh_keys, NT) * scale, -1e30)

    for i in range(1, TP):
        square_arrival(i).wait_recv()
    total = jnp.sum(squares[...].reshape(TP, ROWS), axis=0, keepdims=True)
    inverse_rms[...] = jnp.broadcast_to(lax.rsqrt(total / D + EPSILON), (HD, ROWS)).T

    schedules = {
        0: [(1, 0, 0), (1, 0, 1)],
        1: [(0, 3, 0), (0, 3, 1), (1, 0, 0), (0, 2, 0), (1, 0, 1), (0, 2, 1), (1, 1, 0), (1, 1, 1), (0, 1, 0), (0, 1, 1)],
        2: [(1, 0, 0), (1, 0, 1), (0, 3, 0), (1, 1, 0), (0, 3, 1), (1, 1, 1), (0, 2, 0), (0, 2, 1), (1, 2, 0), (1, 2, 1)],
        3: [(0, 3, 0), (0, 3, 1)],
    }
    for here in range(CHIPS):
        @pl.when(chip == here)
        def _(here=here):
            have = {0: {3, 2, 1}, 3: {0, 1, 2}}.get(here, set())
            begun = set()
            for way, place, h in schedules[here]:
                if place not in have:
                    have.add(place)
                    pair_copy(place).wait_recv()
                rows = pl.ds(h * HALF, HALF)
                value = final[rows, :] if place == here and h in begun else block(place, h)
                line_copy(way, place, h, tp + 4 * way - 2).wait_recv()
                value = value + landing[way, place, rows].astype(F32)
                if place == here:
                    begun.add(h)
                    final[rows, :] = value
                else:
                    line_out[place, rows] = value.astype(BF16)
                    line_copy(way, place, h, tp + 2 - 4 * way).start()

    @pl.when(tp == LEADER)
    def _():
        pl.semaphore_wait(barrier, GRP - 1)
        lax.fori_loop(1, TP, tell_group, 0)

    keys = final[:, 0:HD] * inverse_rms[...] + bias_ref[0:HD][None, :]
    values = final[:, HD:WIDTH] * inverse_rms[...] + bias_ref[HD:WIDTH][None, :]
    turned = pltpu.roll(keys, HD // 2, 1)
    keys = (keys * cos_rows[...] + turned * sin_rows[...]).astype(BF16)
    handed = jnp.concatenate([keys, values.astype(BF16)], axis=1)

    @pl.when(tp != LEADER)
    def _():
        pl.semaphore_wait(all_in, 1)

    y, x = plane // 4, plane % 4

    def send(away, target_layer):
        def body(i, carry):
            target = (y + i // 4) % 4 * 4 + (x + i % 4) % 4
            pltpu.make_async_remote_copy(
                src_ref=outgoing.at[target_layer, target], dst_ref=arrived.at[layer, plane],
                send_sem=hand_send.at[away], recv_sem=hand_recv.at[away],
                device_id={"grp": target * LAYERS + target_layer}, device_id_type=MESH,
            ).start()
            return carry
        return body

    def handed_over(away):
        blocks = pl.ds(0, PLANE if away else PLANE - 1)
        return pltpu.make_async_remote_copy(
            src_ref=outgoing.at[0, blocks], dst_ref=arrived.at[0, blocks],
            send_sem=hand_send.at[away], recv_sem=hand_recv.at[away],
            device_id={"grp": (group + 1) % GRP}, device_id_type=MESH,
        )

    for away in (2, 1, 3, 0):
        target_layer = (layer + away) % LAYERS
        picked = dot(pick[target_layer], handed).astype(BF16)
        outgoing[pl.ds(target_layer, 1)] = picked.reshape(1, PLANE, SLOT, WIDTH)
        lax.fori_loop(0 if away else 1, PLANE, send(away, target_layer), 0)
    arrived[pl.ds(layer, 1), pl.ds(plane, 1)] = outgoing[pl.ds(layer, 1), pl.ds(plane, 1)]

    for away in (0, 1, 3, 2):
        handed_over(away).wait_recv()
        z = (layer + LAYERS - away) % LAYERS
        span_live = live[z] > 0.5
        for half in range(2):
            eight = pl.ds(half * 8, 8)
            asked = query[z, eight].reshape(128, HD)
            old_values = old[z, eight, :, HD:WIDTH].reshape(128, HD)
            span_keys = arrived[z, eight, :, 0:HD].reshape(128, HD)
            span_values = arrived[z, eight, :, HD:WIDTH].reshape(128, HD)
            fresh_values = new_values[pl.ds(pl.multiple_of(z * 64 + half * 32, 32), 32), :]
            cached, fresh = score_old[2 * z + half], score_new[2 * z + half]
            may = same & span_live[:, half * 128:half * 128 + 128]
            span = jnp.where(may, dot(asked, span_keys, NT) * scale, -1e30)
            top = jnp.max(jnp.maximum(cached, span), axis=1, keepdims=True)
            top = jnp.maximum(top, jnp.max(fresh, axis=1, keepdims=True))
            cached, span, fresh = jnp.exp(cached - top), jnp.exp(span - top), jnp.exp(fresh - top)
            weight_sum = jnp.sum(cached + span, axis=1, keepdims=True) + jnp.sum(fresh, axis=1, keepdims=True)
            inverse = 1.0 / weight_sum
            result = dot((cached * inverse).astype(BF16), old_values)
            result = result + dot((span * inverse).astype(BF16), span_values)
            result = result + dot((fresh * inverse).astype(BF16), fresh_values)
            out_ref[eight, pl.ds(z, 1)] = result.astype(BF16).reshape(8, 1, SLOT, HD)

    for place in range(CHIPS):
        pair_copy(place).wait_send()
        for h in range(2):
            @pl.when(chip != place)
            def _(place=place, h=h):
                line_copy(0, place, h, partner).wait_send()
    for i in range(1, TP):
        square_copy(i).wait_send()
    for away in (0, 1, 3, 2):
        handed_over(away).wait_send()


def shards(tokens, gain, kv_weight, kv_bias, lengths, dest, queries, old_cache, new_kv):
    query_rows = queries.reshape(GRP, STEPS, QPK, HD).transpose(0, 2, 1, 3).reshape(PLANE, LAYERS, SLOT, HD)
    new_rows = new_kv.reshape(GRP, STEPS, 2, HD).transpose(0, 2, 1, 3).reshape(4 * GRP, HD)
    any_space = pl.BlockSpec(memory_space=pl.ANY)
    vmem = pl.BlockSpec(memory_space=pltpu.VMEM)
    dma = pltpu.SemaphoreType.DMA
    out = pl.pallas_call(
        kernel,
        out_shape=jax.ShapeDtypeStruct((PLANE, LAYERS, SLOT, HD), BF16),
        in_specs=[any_space] * 10,
        out_specs=vmem,
        scratch_shapes=[
            pltpu.VMEM((ROWS, FEATS), BF16),
            pltpu.VMEM((ROWS, FEATS), BF16),
            pltpu.VMEM((TP, FEATS, WIDTH), BF16),
            pltpu.VMEM((FEATS,), F32),
            pltpu.VMEM((WIDTH,), F32),
            pltpu.VMEM((GRP, GRP), jnp.int32),
            pltpu.VMEM((GRP, GRP), jnp.int32),
            pltpu.VMEM((LAYERS, PLANE, SLOT, HD), BF16),
            pltpu.VMEM((LAYERS, PLANE, SLOT, WIDTH), BF16),
            pltpu.VMEM((4 * GRP, HD), BF16),
            pltpu.VMEM((4 * GRP, HD), BF16),
            pltpu.VMEM((4 * GRP, HD), BF16),
            pltpu.VMEM((SLOT, 2 * HD), F32),
            pltpu.VMEM((CHIPS, ROWS, WIDTH), BF16),
            pltpu.VMEM((CHIPS, ROWS, WIDTH), BF16),
            pltpu.VMEM((CHIPS, ROWS, WIDTH), F32),
            pltpu.VMEM((2, CHIPS, ROWS, WIDTH), BF16),
            pltpu.VMEM((CHIPS, ROWS, WIDTH), BF16),
            pltpu.VMEM((ROWS, WIDTH), F32),
            pltpu.VMEM((TP, 1, ROWS), F32),
            pltpu.VMEM((LAYERS, LANES, ROWS), BF16),
            pltpu.VMEM((ROWS, HD), F32),
            pltpu.VMEM((ROWS, HD), F32),
            pltpu.VMEM((ROWS, HD), F32),
            pltpu.VMEM((LAYERS, 1, LANES), F32),
            pltpu.VMEM((8, 128, 128), F32),
            pltpu.VMEM((8, 128, 32), F32),
            pltpu.VMEM((LAYERS, PLANE, SLOT, WIDTH), BF16),
            pltpu.VMEM((LAYERS, PLANE, SLOT, WIDTH), BF16),
            pltpu.SemaphoreType.REGULAR,
            pltpu.SemaphoreType.REGULAR,
            dma((15,)),
            dma((TP,)),
            dma((TP,)),
            dma((TP,)),
            dma((CHIPS,)),
            dma((CHIPS,)),
            dma((CHIPS, 2)),
            dma((2, CHIPS, 2)),
            dma((LAYERS,)),
            dma((LAYERS,)),
        ],
        compiler_params=pltpu.CompilerParams(
            collective_id=0, has_side_effects=True, vmem_limit_bytes=60 * 1024 * 1024
        ),
        cost_estimate=pl.CostEstimate(flops=2_500_000_000, bytes_accessed=6_000_000, transcendentals=300_000),
    )(
        tokens, kv_weight, gain, kv_bias, lengths, dest,
        query_rows, old_cache.reshape(PLANE, LAYERS, SLOT, WIDTH), new_rows, jnp.asarray(rotary_tables()),
    )
    return out.reshape(GRP, QPK, STEPS, HD).transpose(0, 2, 1, 3).reshape(1, GRP, STEPS, QPK * HD)


def solution(mesh):
    return jax.shard_map(
        shards,
        mesh=mesh,
        in_specs=(
            P("grp", "tp"),
            P("tp"),
            P("tp", None),
            P("tp"),
            P(),
            P(),
            P("grp", None, None, "tp"),
            P("grp", None, None, "tp"),
            P("grp", None, None, "tp"),
        ),
        out_specs=P("grp", None, None, "tp"),
        check_vma=False,
    )
```

```python
import functools
import math

import jax
import jax.numpy as jnp
import numpy as np
from jax import lax
from jax.experimental import pallas as pl
from jax.experimental.pallas import tpu as pltpu
from jax.sharding import PartitionSpec as P

D = 6144
HD = 128
SLOT = 16
CACHED = 16
STEPS = 2
KVW = 2048
QPK = 8
EPSILON = 1e-06
THETA = 1000000.0

ROWS = 512
FEATS = 768
GRP = 64
TP = 8
CHIPS = 4
WIDTH = 256
HALF = ROWS // 2
SLOTS = GRP * SLOT
LAYERS = 4
PLANE = GRP // LAYERS
LANES = PLANE * SLOT
LEADER = 7
MESH = pl.DeviceIdType.MESH
F32 = jnp.float32
BF16 = jnp.bfloat16
NT = (((1,), (1,)), ((), ()))
NN = (((1,), (0,)), ((), ()))


def dot(a, b, dims=NN):
    return lax.dot_general(a, b, dims, preferred_element_type=F32)


def iota(shape, axis):
    return lax.broadcasted_iota(jnp.int32, shape, axis)


def rotary_tables():
    half = HD // 2
    frequency = np.power(np.float32(THETA), -2.0 * np.arange(half, dtype=np.float32) / np.float32(HD)).astype(np.float32)
    angles = ((CACHED + np.arange(SLOT)).astype(np.float32)[:, None] * frequency[None, :]).astype(np.float32)
    cosine, sine = np.cos(angles), np.sin(angles)
    return np.concatenate([cosine, cosine, -sine, sine], axis=1).astype(np.float32)


def kernel(
    tokens_hbm, weight_hbm, gain_hbm, bias_hbm, lengths_hbm, dest_hbm, query_hbm, old_hbm, new_hbm, table_hbm,
    out_ref,
    tokens, scaled, weight, gain_ref, bias_ref, lengths_ref, dest_ref, query, old, new_ref, new_keys, new_values, table_ref,
    pair_out, pair_in, own, landing, line_out, final,
    squares, pick, cos_rows, sin_rows, inverse_rms, live, score_old, score_new, outgoing, arrived,
    joined, all_in,
    load_sem, weight_sem, sq_send, sq_recv, pair_send, pair_recv, line_send, line_recv, hand_send, hand_recv,
):
    group = lax.axis_index("grp")
    tp = lax.axis_index("tp")
    chip = tp // 2
    core = tp % 2
    partner = tp + 1 - 2 * core
    plane, layer = group // LAYERS, group % LAYERS

    load_gain = pltpu.make_async_copy(gain_hbm, gain_ref, load_sem.at[0])
    load_tokens = pltpu.make_async_copy(tokens_hbm, tokens, load_sem.at[1])
    load_gain.start()
    load_tokens.start()

    def head_of(step, whose):
        place = jnp.where(chip < 2, CHIPS - 1 - step, step)
        return place, 2 * place + whose

    def load_weight(step, which):
        whose = (1 - core) if which == 0 else core
        _, head = head_of(step, whose)
        columns = pl.ds(pl.multiple_of(head * WIDTH, WIDTH), WIDTH)
        return pltpu.make_async_copy(weight_hbm.at[:, columns], weight.at[4 * which + step], weight_sem.at[4 * which + step])

    for step in range(CHIPS):
        for which in range(2):
            load_weight(step, which).start()
    later_loads = [
        (lengths_hbm, lengths_ref), (dest_hbm, dest_ref), (table_hbm, table_ref), (bias_hbm, bias_ref), (new_hbm, new_ref),
    ]
    for z in range(LAYERS):
        later_loads.append((query_hbm.at[:, z], query.at[z]))
        later_loads.append((old_hbm.at[:, z], old.at[z]))
    later_loads = [
        pltpu.make_async_copy(source, target, load_sem.at[2 + i]) for i, (source, target) in enumerate(later_loads)
    ]

    barrier = pltpu.get_barrier_semaphore()

    def greet_tp(i, carry):
        peer = (tp + i) % TP

        @pl.when(peer != LEADER)
        def _():
            pl.semaphore_signal(barrier, inc=1, device_id={"tp": peer}, device_id_type=MESH)

        return carry

    def greet_leaders(i, carry):
        pl.semaphore_signal(barrier, inc=1, device_id={"grp": (group + i) % GRP}, device_id_type=MESH)
        return carry

    def tell_group(i, carry):
        pl.semaphore_signal(all_in, inc=1, device_id={"tp": (tp + i) % TP}, device_id_type=MESH)
        return carry

    lax.fori_loop(1, TP, greet_tp, 0)

    @pl.when(tp != LEADER)
    def _():
        pl.semaphore_wait(barrier, TP - 1)
        pl.semaphore_signal(joined, inc=1, device_id={"tp": LEADER}, device_id_type=MESH)

    load_gain.wait()
    load_tokens.wait()
    for h in range(2):
        rows = pl.ds(h * HALF, HALF)
        scaled[rows, :] = (tokens[rows, :].astype(F32) * gain_ref[...][None, :]).astype(BF16)

    def pair_copy(place):
        return pltpu.make_async_remote_copy(
            src_ref=pair_out.at[place], dst_ref=pair_in.at[place],
            send_sem=pair_send.at[place], recv_sem=pair_recv.at[place],
            device_id={"tp": partner}, device_id_type=MESH,
        )

    def line_copy(way, place, h, to):
        rows = pl.ds(h * HALF, HALF)
        return pltpu.make_async_remote_copy(
            src_ref=line_out.at[place, rows], dst_ref=landing.at[way, place, rows],
            send_sem=line_send.at[place, h], recv_sem=line_recv.at[way, place, h],
            device_id={"tp": to}, device_id_type=MESH,
        )

    def block(place, h):
        rows = pl.ds(h * HALF, HALF)
        return own[place, rows] + pair_in[place, rows].astype(F32)

    def multiply_pair(step):
        place, _ = head_of(step, 0)
        load_weight(step, 0).wait()
        pair_out[pl.ds(place, 1)] = dot(scaled[...], weight[step]).astype(BF16)[None]
        if step == 0:
            @pl.when(tp == LEADER)
            def _():
                pl.semaphore_wait(joined, TP - 1)
                lax.fori_loop(1, GRP, greet_leaders, 0)
        pair_copy(place).start()

    def multiply_own(step):
        place, _ = head_of(step, 0)
        load_weight(step, 1).wait()
        own[pl.ds(place, 1)] = dot(scaled[...], weight[4 + step])[None]

    def first_sends(step):
        place, _ = head_of(step, 0)
        way = chip // (CHIPS - 1)

        @pl.when(chip % (CHIPS - 1) == 0)
        def _():
            pair_copy(place).wait_recv()
            for h in range(2):
                rows = pl.ds(h * HALF, HALF)
                line_out[place, rows] = block(place, h).astype(BF16)
                line_copy(way, place, h, tp + 2 - 4 * way).start()

    for load in later_loads:
        load.start()
    for step in range(CHIPS):
        multiply_pair(step)

    def square_copy(i):
        return pltpu.make_async_remote_copy(
            src_ref=squares.at[tp], dst_ref=squares.at[tp],
            send_sem=sq_send.at[i], recv_sem=sq_recv.at[tp],
            device_id={"tp": (tp + i) % TP}, device_id_type=MESH,
        )

    def square_arrival(i):
        source = (tp + i) % TP
        return pltpu.make_async_remote_copy(
            src_ref=squares.at[source], dst_ref=squares.at[source],
            send_sem=sq_send.at[i], recv_sem=sq_recv.at[source],
            device_id={"tp": source}, device_id_type=MESH,
        )

    for h in range(2):
        floats = tokens[pl.ds(h * HALF, HALF), :].astype(F32)
        square = floats * floats
        high = square.astype(BF16)
        low = (square - high.astype(F32)).astype(BF16)
        ones = jnp.ones((8, FEATS), BF16)
        sums = dot(ones, high, NT) + dot(ones, low, NT)
        squares[pl.ds(tp, 1), :, h * HALF:(h + 1) * HALF] = sums[0:1, :].reshape(1, 1, HALF)
    for i in range(1, TP):
        square_copy(i).start()

    for step in range(CHIPS):
        multiply_own(step)
        if step < CHIPS - 1:
            first_sends(step)

    for load in later_loads:
        load.wait()
    lengths = lengths_ref[...]
    dests = dest_ref[...]
    mine = iota((GRP, GRP), 0) == group
    own_lengths = jnp.sum(jnp.where(mine, lengths, 0), axis=0, keepdims=True)
    own_dest = jnp.sum(jnp.where(mine, dests, 0), axis=0, keepdims=True)
    before = (iota((GRP, GRP), 0) < iota((GRP, GRP), 1)).astype(F32)
    spread = jnp.broadcast_to(own_lengths.astype(F32), (8, GRP))
    starts = dot(spread, before)[0:1, :].astype(jnp.int32)
    by_layer = iota((GRP, GRP), 0) % PLANE * LAYERS + iota((GRP, GRP), 0) // PLANE
    routed = own_dest == by_layer
    slot_first = jnp.sum(jnp.where(routed, starts, 0), axis=1, keepdims=True)
    slot_length = jnp.sum(jnp.where(routed, own_lengths, 0), axis=1, keepdims=True)
    for part in range(8):
        requests = slice(part * 8, part * 8 + 8)
        offset = iota((8, SLOT, ROWS), 1)
        first = slot_first[requests][:, :, None]
        length = slot_length[requests][:, :, None]
        hit = (iota((8, SLOT, ROWS), 2) == first + offset) & (offset < length)
        pick[part // 2, part % 2 * 128:part % 2 * 128 + 128, :] = hit.astype(F32).reshape(128, ROWS).astype(BF16)

    row_index = iota((ROWS, GRP), 0)
    first_row = jnp.max(jnp.where(starts <= row_index, starts, 0), axis=1, keepdims=True)
    at_offset = (iota((ROWS, SLOT), 1) + first_row == iota((ROWS, SLOT), 0)).astype(F32).astype(BF16)
    rest = table_ref[...]
    tabled = jnp.zeros((ROWS, 2 * HD), F32)
    for _ in range(3):
        term = rest.astype(BF16)
        rest = rest - term.astype(F32)
        tabled = tabled + dot(at_offset, term)
    cos_rows[...] = tabled[:, 0:HD]
    sin_rows[...] = tabled[:, HD:2 * HD]

    live_rows = jnp.sum(jnp.where(dests == group, lengths, 0), axis=1, keepdims=True)
    for z in range(LAYERS):
        at_source = iota((GRP, LANES), 1) // SLOT * LAYERS + z == iota((GRP, LANES), 0)
        live_lanes = jnp.sum(jnp.where(at_source, live_rows, 0), axis=0, keepdims=True)
        live[z] = (iota((1, LANES), 1) % SLOT < live_lanes).astype(F32)

    sorted_row = iota((4 * GRP, 4 * GRP), 0)
    natural = (sorted_row // 4 % PLANE * LAYERS + sorted_row // (4 * PLANE)) * 4 + sorted_row % 4
    column = iota((4 * GRP, 4 * GRP), 1)
    new_keys[...] = dot((column == natural).astype(F32).astype(BF16), new_ref[...]).astype(BF16)
    shifted = (column == natural + 2) & (sorted_row % 4 < 2)
    new_values[...] = dot(shifted.astype(F32).astype(BF16), new_ref[...]).astype(BF16)

    scale = 1.0 / math.sqrt(HD)
    same = iota((128, 128), 0) // 16 == iota((128, 128), 1) // 16
    same_new = (iota((128, 32), 0) // 16 == iota((128, 32), 1) // 4) & (iota((128, 32), 1) % 4 <= iota((128, 32), 0) % 2)
    for z in range(LAYERS):
        for half in range(2):
            eight = slice(half * 8, half * 8 + 8)
            asked = query[z, eight].reshape(128, HD)
            cached_keys = old[z, eight, :, 0:HD].reshape(128, HD)
            fresh_keys = new_keys[z * 64 + half * 32:z * 64 + half * 32 + 32, :]
            score_old[2 * z + half] = jnp.where(same, dot(asked, cached_keys, NT) * scale, -1e30)
            score_new[2 * z + half] = jnp.where(same_new, dot(asked, fresh_keys, NT) * scale, -1e30)

    schedules = {
        0: [(1, 0, 0), (1, 0, 1)],
        1: [(0, 3, 0), (0, 3, 1), (1, 0, 0), (0, 2, 0), (1, 0, 1), (0, 2, 1), (1, 1, 0), (1, 1, 1), (0, 1, 0), (0, 1, 1)],
        2: [(1, 0, 0), (1, 0, 1), (0, 3, 0), (1, 1, 0), (0, 3, 1), (1, 1, 1), (0, 2, 0), (0, 2, 1), (1, 2, 0), (1, 2, 1)],
        3: [(0, 3, 0), (0, 3, 1)],
    }
    for here in range(CHIPS):
        @pl.when(chip == here)
        def _(here=here):
            have = {0: {3, 2, 1}, 3: {0, 1, 2}}.get(here, set())
            begun = set()
            for way, place, h in schedules[here]:
                if place not in have:
                    have.add(place)
                    pair_copy(place).wait_recv()
                rows = pl.ds(h * HALF, HALF)
                value = final[rows, :] if place == here and h in begun else block(place, h)
                line_copy(way, place, h, tp + 4 * way - 2).wait_recv()
                value = value + landing[way, place, rows].astype(F32)
                if place == here:
                    begun.add(h)
                    final[rows, :] = value
                else:
                    line_out[place, rows] = value.astype(BF16)
                    line_copy(way, place, h, tp + 2 - 4 * way).start()

    @pl.when(tp == LEADER)
    def _():
        pl.semaphore_wait(barrier, GRP - 1)
        lax.fori_loop(1, TP, tell_group, 0)

    for i in range(1, TP):
        square_arrival(i).wait_recv()
    total = jnp.sum(squares[...].reshape(TP, ROWS), axis=0, keepdims=True)
    inverse_rms[...] = jnp.broadcast_to(lax.rsqrt(total / D + EPSILON), (HD, ROWS)).T
    keys = final[:, 0:HD] * inverse_rms[...] + bias_ref[0:HD][None, :]
    values = final[:, HD:WIDTH] * inverse_rms[...] + bias_ref[HD:WIDTH][None, :]
    turned = pltpu.roll(keys, HD // 2, 1)
    keys = (keys * cos_rows[...] + turned * sin_rows[...]).astype(BF16)
    handed = jnp.concatenate([keys, values.astype(BF16)], axis=1)

    @pl.when(tp != LEADER)
    def _():
        pl.semaphore_wait(all_in, 1)

    y, x = plane // 4, plane % 4

    def send(aways):
        def body(i, carry):
            target = (y + i // 4) % 4 * 4 + (x + i % 4) % 4
            for away in aways:
                target_layer = (layer + away) % LAYERS
                copy = pltpu.make_async_remote_copy(
                    src_ref=outgoing.at[target_layer, target], dst_ref=arrived.at[layer, plane],
                    send_sem=hand_send.at[away], recv_sem=hand_recv.at[away],
                    device_id={"grp": target * LAYERS + target_layer}, device_id_type=MESH,
                )
                if away:
                    copy.start()
                else:
                    pl.when(i > 0)(copy.start)
            return carry
        return body

    def handed_over(away):
        blocks = pl.ds(0, PLANE if away else PLANE - 1)
        return pltpu.make_async_remote_copy(
            src_ref=outgoing.at[0, blocks], dst_ref=arrived.at[0, blocks],
            send_sem=hand_send.at[away], recv_sem=hand_recv.at[away],
            device_id={"grp": (group + 1) % GRP}, device_id_type=MESH,
        )

    for aways in ((1, 3), (2,), (0,)):
        for away in aways:
            target_layer = (layer + away) % LAYERS
            picked = dot(pick[target_layer], handed).astype(BF16)
            outgoing[pl.ds(target_layer, 1)] = picked.reshape(1, PLANE, SLOT, WIDTH)
        lax.fori_loop(0, PLANE, send(aways), 0)
    arrived[pl.ds(layer, 1), pl.ds(plane, 1)] = outgoing[pl.ds(layer, 1), pl.ds(plane, 1)]

    for away in (0, 1, 3, 2):
        handed_over(away).wait_recv()
        z = (layer + LAYERS - away) % LAYERS
        span_live = live[z] > 0.5
        for half in range(2):
            eight = pl.ds(half * 8, 8)
            asked = query[z, eight].reshape(128, HD)
            old_values = old[z, eight, :, HD:WIDTH].reshape(128, HD)
            span_keys = arrived[z, eight, :, 0:HD].reshape(128, HD)
            span_values = arrived[z, eight, :, HD:WIDTH].reshape(128, HD)
            fresh_values = new_values[pl.ds(pl.multiple_of(z * 64 + half * 32, 32), 32), :]
            cached, fresh = score_old[2 * z + half], score_new[2 * z + half]
            may = same & span_live[:, half * 128:half * 128 + 128]
            span = jnp.where(may, dot(asked, span_keys, NT) * scale, -1e30)
            top = jnp.max(jnp.maximum(cached, span), axis=1, keepdims=True)
            top = jnp.maximum(top, jnp.max(fresh, axis=1, keepdims=True))
            cached, span, fresh = jnp.exp(cached - top), jnp.exp(span - top), jnp.exp(fresh - top)
            weight_sum = jnp.sum(cached + span, axis=1, keepdims=True) + jnp.sum(fresh, axis=1, keepdims=True)
            inverse = 1.0 / weight_sum
            result = dot((cached * inverse).astype(BF16), old_values)
            result = result + dot((span * inverse).astype(BF16), span_values)
            result = result + dot((fresh * inverse).astype(BF16), fresh_values)
            out_ref[eight, pl.ds(z, 1)] = result.astype(BF16).reshape(8, 1, SLOT, HD)

    for place in range(CHIPS):
        pair_copy(place).wait_send()
        for h in range(2):
            @pl.when(chip != place)
            def _(place=place, h=h):
                line_copy(0, place, h, partner).wait_send()
    for i in range(1, TP):
        square_copy(i).wait_send()
    for away in (0, 1, 3, 2):
        handed_over(away).wait_send()


def shards(tokens, gain, kv_weight, kv_bias, lengths, dest, queries, old_cache, new_kv):
    query_rows = queries.reshape(GRP, STEPS, QPK, HD).transpose(0, 2, 1, 3).reshape(PLANE, LAYERS, SLOT, HD)
    new_rows = new_kv.reshape(GRP, STEPS, 2, HD).transpose(0, 2, 1, 3).reshape(4 * GRP, HD)
    any_space = pl.BlockSpec(memory_space=pl.ANY)
    vmem = pl.BlockSpec(memory_space=pltpu.VMEM)
    dma = pltpu.SemaphoreType.DMA
    out = pl.pallas_call(
        kernel,
        out_shape=jax.ShapeDtypeStruct((PLANE, LAYERS, SLOT, HD), BF16),
        in_specs=[any_space] * 10,
        out_specs=vmem,
        scratch_shapes=[
            pltpu.VMEM((ROWS, FEATS), BF16),
            pltpu.VMEM((ROWS, FEATS), BF16),
            pltpu.VMEM((TP, FEATS, WIDTH), BF16),
            pltpu.VMEM((FEATS,), F32),
            pltpu.VMEM((WIDTH,), F32),
            pltpu.VMEM((GRP, GRP), jnp.int32),
            pltpu.VMEM((GRP, GRP), jnp.int32),
            pltpu.VMEM((LAYERS, PLANE, SLOT, HD), BF16),
            pltpu.VMEM((LAYERS, PLANE, SLOT, WIDTH), BF16),
            pltpu.VMEM((4 * GRP, HD), BF16),
            pltpu.VMEM((4 * GRP, HD), BF16),
            pltpu.VMEM((4 * GRP, HD), BF16),
            pltpu.VMEM((SLOT, 2 * HD), F32),
            pltpu.VMEM((CHIPS, ROWS, WIDTH), BF16),
            pltpu.VMEM((CHIPS, ROWS, WIDTH), BF16),
            pltpu.VMEM((CHIPS, ROWS, WIDTH), F32),
            pltpu.VMEM((2, CHIPS, ROWS, WIDTH), BF16),
            pltpu.VMEM((CHIPS, ROWS, WIDTH), BF16),
            pltpu.VMEM((ROWS, WIDTH), F32),
            pltpu.VMEM((TP, 1, ROWS), F32),
            pltpu.VMEM((LAYERS, LANES, ROWS), BF16),
            pltpu.VMEM((ROWS, HD), F32),
            pltpu.VMEM((ROWS, HD), F32),
            pltpu.VMEM((ROWS, HD), F32),
            pltpu.VMEM((LAYERS, 1, LANES), F32),
            pltpu.VMEM((8, 128, 128), F32),
            pltpu.VMEM((8, 128, 32), F32),
            pltpu.VMEM((LAYERS, PLANE, SLOT, WIDTH), BF16),
            pltpu.VMEM((LAYERS, PLANE, SLOT, WIDTH), BF16),
            pltpu.SemaphoreType.REGULAR,
            pltpu.SemaphoreType.REGULAR,
            dma((15,)),
            dma((TP,)),
            dma((TP,)),
            dma((TP,)),
            dma((CHIPS,)),
            dma((CHIPS,)),
            dma((CHIPS, 2)),
            dma((2, CHIPS, 2)),
            dma((LAYERS,)),
            dma((LAYERS,)),
        ],
        compiler_params=pltpu.CompilerParams(
            collective_id=0, has_side_effects=True, vmem_limit_bytes=60 * 1024 * 1024
        ),
        cost_estimate=pl.CostEstimate(flops=2_500_000_000, bytes_accessed=6_000_000, transcendentals=300_000),
    )(
        tokens, kv_weight, gain, kv_bias, lengths, dest,
        query_rows, old_cache.reshape(PLANE, LAYERS, SLOT, WIDTH), new_rows, jnp.asarray(rotary_tables()),
    )
    return out.reshape(GRP, QPK, STEPS, HD).transpose(0, 2, 1, 3).reshape(1, GRP, STEPS, QPK * HD)


def solution(mesh):
    return jax.shard_map(
        shards,
        mesh=mesh,
        in_specs=(
            P("grp", "tp"),
            P("tp"),
            P("tp", None),
            P("tp"),
            P(),
            P(),
            P("grp", None, None, "tp"),
            P("grp", None, None, "tp"),
            P("grp", None, None, "tp"),
        ),
        out_specs=P("grp", None, None, "tp"),
        check_vma=False,
    )
```

```python
import functools
import math

import jax
import jax.numpy as jnp
import numpy as np
from jax import lax
from jax.experimental import pallas as pl
from jax.experimental.pallas import tpu as pltpu
from jax.sharding import PartitionSpec as P

D = 6144
HD = 128
SLOT = 16
CACHED = 16
STEPS = 2
KVW = 2048
QPK = 8
EPSILON = 1e-06
THETA = 1000000.0

ROWS = 512
FEATS = 768
GRP = 64
TP = 8
CHIPS = 4
WIDTH = 256
HALF = ROWS // 2
SLOTS = GRP * SLOT
LAYERS = 4
PLANE = GRP // LAYERS
LANES = PLANE * SLOT
LEADER = 7
MESH = pl.DeviceIdType.MESH
F32 = jnp.float32
BF16 = jnp.bfloat16
NT = (((1,), (1,)), ((), ()))
NN = (((1,), (0,)), ((), ()))


def dot(a, b, dims=NN):
    return lax.dot_general(a, b, dims, preferred_element_type=F32)


def iota(shape, axis):
    return lax.broadcasted_iota(jnp.int32, shape, axis)


def rotary_tables():
    half = HD // 2
    frequency = np.power(np.float32(THETA), -2.0 * np.arange(half, dtype=np.float32) / np.float32(HD)).astype(np.float32)
    angles = ((CACHED + np.arange(SLOT)).astype(np.float32)[:, None] * frequency[None, :]).astype(np.float32)
    cosine, sine = np.cos(angles), np.sin(angles)
    return np.concatenate([cosine, cosine, -sine, sine], axis=1).astype(np.float32)


def kernel(
    tokens_hbm, weight_hbm, gain_hbm, bias_hbm, lengths_hbm, dest_hbm, query_hbm, old_hbm, new_hbm, table_hbm,
    out_ref,
    tokens, scaled, weight, gain_ref, bias_ref, lengths_ref, dest_ref, query, old, new_ref, new_keys, new_values, table_ref,
    pair_out, pair_in, own, landing, line_out, final, handed,
    squares, pick, cos_rows, sin_rows, inverse_rms, live, score_old, score_new, outgoing, arrived,
    joined, all_in,
    load_sem, weight_sem, sq_send, sq_recv, pair_send, pair_recv, line_send, line_recv, hand_send, hand_recv,
):
    group = lax.axis_index("grp")
    tp = lax.axis_index("tp")
    chip = tp // 2
    core = tp % 2
    partner = tp + 1 - 2 * core
    plane, layer = group // LAYERS, group % LAYERS

    load_gain = pltpu.make_async_copy(gain_hbm, gain_ref, load_sem.at[0])
    load_tokens = pltpu.make_async_copy(tokens_hbm, tokens, load_sem.at[1])
    load_gain.start()
    load_tokens.start()

    def head_of(step, whose):
        place = jnp.where(chip < 2, CHIPS - 1 - step, step)
        return place, 2 * place + whose

    def load_weight(step, which):
        whose = (1 - core) if which == 0 else core
        _, head = head_of(step, whose)
        columns = pl.ds(pl.multiple_of(head * WIDTH, WIDTH), WIDTH)
        return pltpu.make_async_copy(weight_hbm.at[:, columns], weight.at[4 * which + step], weight_sem.at[4 * which + step])

    for step in range(CHIPS):
        for which in range(2):
            load_weight(step, which).start()
    later_loads = [
        (lengths_hbm, lengths_ref), (dest_hbm, dest_ref), (table_hbm, table_ref), (bias_hbm, bias_ref), (new_hbm, new_ref),
    ]
    for z in range(LAYERS):
        later_loads.append((query_hbm.at[:, z], query.at[z]))
        later_loads.append((old_hbm.at[:, z], old.at[z]))
    later_loads = [
        pltpu.make_async_copy(source, target, load_sem.at[2 + i]) for i, (source, target) in enumerate(later_loads)
    ]

    barrier = pltpu.get_barrier_semaphore()

    def greet_tp(i, carry):
        peer = (tp + i) % TP

        @pl.when(peer != LEADER)
        def _():
            pl.semaphore_signal(barrier, inc=1, device_id={"tp": peer}, device_id_type=MESH)

        return carry

    def greet_leaders(i, carry):
        pl.semaphore_signal(barrier, inc=1, device_id={"grp": (group + i) % GRP}, device_id_type=MESH)
        return carry

    def tell_group(i, carry):
        pl.semaphore_signal(all_in, inc=1, device_id={"tp": (tp + i) % TP}, device_id_type=MESH)
        return carry

    lax.fori_loop(1, TP, greet_tp, 0)

    @pl.when(tp != LEADER)
    def _():
        pl.semaphore_wait(barrier, TP - 1)
        pl.semaphore_signal(joined, inc=1, device_id={"tp": LEADER}, device_id_type=MESH)

    load_gain.wait()
    load_tokens.wait()
    for h in range(2):
        rows = pl.ds(h * HALF, HALF)
        scaled[rows, :] = (tokens[rows, :].astype(F32) * gain_ref[...][None, :]).astype(BF16)

    def pair_copy(place):
        return pltpu.make_async_remote_copy(
            src_ref=pair_out.at[place], dst_ref=pair_in.at[place],
            send_sem=pair_send.at[place], recv_sem=pair_recv.at[place],
            device_id={"tp": partner}, device_id_type=MESH,
        )

    def line_copy(way, place, h, to):
        rows = pl.ds(h * HALF, HALF)
        return pltpu.make_async_remote_copy(
            src_ref=line_out.at[place, rows], dst_ref=landing.at[way, place, rows],
            send_sem=line_send.at[place, h], recv_sem=line_recv.at[way, place, h],
            device_id={"tp": to}, device_id_type=MESH,
        )

    def block(place, h):
        rows = pl.ds(h * HALF, HALF)
        return own[place, rows] + pair_in[place, rows].astype(F32)

    def multiply_pair(step):
        place, _ = head_of(step, 0)
        load_weight(step, 0).wait()
        pair_out[pl.ds(place, 1)] = dot(scaled[...], weight[step]).astype(BF16)[None]
        if step == 0:
            @pl.when(tp == LEADER)
            def _():
                pl.semaphore_wait(joined, TP - 1)
                lax.fori_loop(1, GRP, greet_leaders, 0)
        pair_copy(place).start()

    def multiply_own(step):
        place, _ = head_of(step, 0)
        load_weight(step, 1).wait()
        own[pl.ds(place, 1)] = dot(scaled[...], weight[4 + step])[None]

    def first_sends(step):
        place, _ = head_of(step, 0)
        way = chip // (CHIPS - 1)

        @pl.when(chip % (CHIPS - 1) == 0)
        def _():
            pair_copy(place).wait_recv()
            for h in range(2):
                rows = pl.ds(h * HALF, HALF)
                line_out[place, rows] = block(place, h).astype(BF16)
                line_copy(way, place, h, tp + 2 - 4 * way).start()

    for load in later_loads:
        load.start()
    def square_copy(i):
        return pltpu.make_async_remote_copy(
            src_ref=squares.at[tp], dst_ref=squares.at[tp],
            send_sem=sq_send.at[i], recv_sem=sq_recv.at[tp],
            device_id={"tp": (tp + i) % TP}, device_id_type=MESH,
        )

    def square_arrival(i):
        source = (tp + i) % TP
        return pltpu.make_async_remote_copy(
            src_ref=squares.at[source], dst_ref=squares.at[source],
            send_sem=sq_send.at[i], recv_sem=sq_recv.at[source],
            device_id={"tp": source}, device_id_type=MESH,
        )

    multiply_pair(0)
    multiply_pair(1)
    multiply_own(0)
    first_sends(0)
    for h in range(2):
        floats = tokens[pl.ds(h * HALF, HALF), :].astype(F32)
        square = floats * floats
        high = square.astype(BF16)
        low = (square - high.astype(F32)).astype(BF16)
        ones = jnp.ones((8, FEATS), BF16)
        sums = dot(ones, high, NT) + dot(ones, low, NT)
        squares[pl.ds(tp, 1), :, h * HALF:(h + 1) * HALF] = sums[0:1, :].reshape(1, 1, HALF)
    for i in range(1, TP):
        square_copy(i).start()
    multiply_pair(2)
    multiply_own(1)
    first_sends(1)
    multiply_pair(3)
    multiply_own(2)
    first_sends(2)
    multiply_own(3)

    for load in later_loads:
        load.wait()
    lengths = lengths_ref[...]
    dests = dest_ref[...]
    mine = iota((GRP, GRP), 0) == group
    own_lengths = jnp.sum(jnp.where(mine, lengths, 0), axis=0, keepdims=True)
    own_dest = jnp.sum(jnp.where(mine, dests, 0), axis=0, keepdims=True)
    before = (iota((GRP, GRP), 0) < iota((GRP, GRP), 1)).astype(F32)
    spread = jnp.broadcast_to(own_lengths.astype(F32), (8, GRP))
    starts = dot(spread, before)[0:1, :].astype(jnp.int32)
    by_layer = iota((GRP, GRP), 0) % PLANE * LAYERS + iota((GRP, GRP), 0) // PLANE
    routed = own_dest == by_layer
    slot_first = jnp.sum(jnp.where(routed, starts, 0), axis=1, keepdims=True)
    slot_length = jnp.sum(jnp.where(routed, own_lengths, 0), axis=1, keepdims=True)
    for part in range(8):
        requests = slice(part * 8, part * 8 + 8)
        offset = iota((8, SLOT, ROWS), 1)
        first = slot_first[requests][:, :, None]
        length = slot_length[requests][:, :, None]
        hit = (iota((8, SLOT, ROWS), 2) == first + offset) & (offset < length)
        pick[part // 2, part % 2 * 128:part % 2 * 128 + 128, :] = hit.astype(F32).reshape(128, ROWS).astype(BF16)

    row_index = iota((ROWS, GRP), 0)
    first_row = jnp.max(jnp.where(starts <= row_index, starts, 0), axis=1, keepdims=True)
    at_offset = (iota((ROWS, SLOT), 1) + first_row == iota((ROWS, SLOT), 0)).astype(F32).astype(BF16)
    rest = table_ref[...]
    tabled = jnp.zeros((ROWS, 2 * HD), F32)
    for _ in range(3):
        term = rest.astype(BF16)
        rest = rest - term.astype(F32)
        tabled = tabled + dot(at_offset, term)
    cos_rows[...] = tabled[:, 0:HD]
    sin_rows[...] = tabled[:, HD:2 * HD]

    live_rows = jnp.sum(jnp.where(dests == group, lengths, 0), axis=1, keepdims=True)
    for z in range(LAYERS):
        at_source = iota((GRP, LANES), 1) // SLOT * LAYERS + z == iota((GRP, LANES), 0)
        live_lanes = jnp.sum(jnp.where(at_source, live_rows, 0), axis=0, keepdims=True)
        live[z] = (iota((1, LANES), 1) % SLOT < live_lanes).astype(F32)

    sorted_row = iota((4 * GRP, 4 * GRP), 0)
    natural = (sorted_row // 4 % PLANE * LAYERS + sorted_row // (4 * PLANE)) * 4 + sorted_row % 4
    column = iota((4 * GRP, 4 * GRP), 1)
    new_keys[...] = dot((column == natural).astype(F32).astype(BF16), new_ref[...]).astype(BF16)
    shifted = (column == natural + 2) & (sorted_row % 4 < 2)
    new_values[...] = dot(shifted.astype(F32).astype(BF16), new_ref[...]).astype(BF16)

    scale = 1.0 / math.sqrt(HD)
    same = iota((128, 128), 0) // 16 == iota((128, 128), 1) // 16
    same_new = (iota((128, 32), 0) // 16 == iota((128, 32), 1) // 4) & (iota((128, 32), 1) % 4 <= iota((128, 32), 0) % 2)
    for z in range(LAYERS):
        for half in range(2):
            eight = slice(half * 8, half * 8 + 8)
            asked = query[z, eight].reshape(128, HD)
            cached_keys = old[z, eight, :, 0:HD].reshape(128, HD)
            fresh_keys = new_keys[z * 64 + half * 32:z * 64 + half * 32 + 32, :]
            score_old[2 * z + half] = jnp.where(same, dot(asked, cached_keys, NT) * scale, -1e30)
            score_new[2 * z + half] = jnp.where(same_new, dot(asked, fresh_keys, NT) * scale, -1e30)

    schedules = {
        0: [(1, 0, 0), (1, 0, 1)],
        1: [(0, 3, 0), (0, 3, 1), (1, 0, 0), (0, 2, 0), (1, 0, 1), (0, 2, 1), (1, 1, 0), (1, 1, 1), (0, 1, 0), (0, 1, 1)],
        2: [(1, 0, 0), (1, 0, 1), (0, 3, 0), (1, 1, 0), (0, 3, 1), (1, 1, 1), (0, 2, 0), (0, 2, 1), (1, 2, 0), (1, 2, 1)],
        3: [(0, 3, 0), (0, 3, 1)],
    }
    have = {0: {3, 2, 1}, 1: set(), 2: set(), 3: {0, 1, 2}}
    begun = {here: set() for here in range(CHIPS)}

    def follow(here, events):
        for way, place, h in events:
            if place not in have[here]:
                have[here].add(place)
                pair_copy(place).wait_recv()
            rows = pl.ds(h * HALF, HALF)
            value = final[rows, :] if place == here and h in begun[here] else block(place, h)
            line_copy(way, place, h, tp + 4 * way - 2).wait_recv()
            value = value + landing[way, place, rows].astype(F32)
            if place == here:
                begun[here].add(h)
                final[rows, :] = value
            else:
                line_out[place, rows] = value.astype(BF16)
                line_copy(way, place, h, tp + 2 - 4 * way).start()

    def finish(h):
        rows = pl.ds(h * HALF, HALF)
        inverse = inverse_rms[rows, :]
        keys = final[rows, 0:HD] * inverse + bias_ref[0:HD][None, :]
        values = final[rows, HD:WIDTH] * inverse + bias_ref[HD:WIDTH][None, :]
        turned = pltpu.roll(keys, HD // 2, 1)
        handed[rows, 0:HD] = (keys * cos_rows[rows, :] + turned * sin_rows[rows, :]).astype(BF16)
        handed[rows, HD:WIDTH] = values.astype(BF16)

    @pl.when(tp == LEADER)
    def _():
        pl.semaphore_wait(barrier, GRP - 1)
        lax.fori_loop(1, TP, tell_group, 0)

    for here in range(CHIPS):
        pl.when(chip == here)(functools.partial(follow, here, schedules[here][:-1]))
    for i in range(1, TP):
        square_arrival(i).wait_recv()
    total = jnp.sum(squares[...].reshape(TP, ROWS), axis=0, keepdims=True)
    inverse_rms[...] = jnp.broadcast_to(lax.rsqrt(total / D + EPSILON), (HD, ROWS)).T
    finish(0)

    @pl.when(tp != LEADER)
    def _():
        pl.semaphore_wait(all_in, 1)

    for here in range(CHIPS):
        pl.when(chip == here)(functools.partial(follow, here, schedules[here][-1:]))
    finish(1)

    y, x = plane // 4, plane % 4

    def send(aways):
        def body(i, carry):
            target = (y + i // 4) % 4 * 4 + (x + i % 4) % 4
            for away in aways:
                target_layer = (layer + away) % LAYERS
                copy = pltpu.make_async_remote_copy(
                    src_ref=outgoing.at[target_layer, target], dst_ref=arrived.at[layer, plane],
                    send_sem=hand_send.at[away], recv_sem=hand_recv.at[away],
                    device_id={"grp": target * LAYERS + target_layer}, device_id_type=MESH,
                )
                if away:
                    copy.start()
                else:
                    pl.when(i > 0)(copy.start)
            return carry
        return body

    def handed_over(away):
        blocks = pl.ds(0, PLANE if away else PLANE - 1)
        return pltpu.make_async_remote_copy(
            src_ref=outgoing.at[0, blocks], dst_ref=arrived.at[0, blocks],
            send_sem=hand_send.at[away], recv_sem=hand_recv.at[away],
            device_id={"grp": (group + 1) % GRP}, device_id_type=MESH,
        )

    for aways in ((1, 3), (2,), (0,)):
        for away in aways:
            target_layer = (layer + away) % LAYERS
            picked = dot(pick[target_layer], handed[...]).astype(BF16)
            outgoing[pl.ds(target_layer, 1)] = picked.reshape(1, PLANE, SLOT, WIDTH)
        lax.fori_loop(0, PLANE, send(aways), 0)
    arrived[pl.ds(layer, 1), pl.ds(plane, 1)] = outgoing[pl.ds(layer, 1), pl.ds(plane, 1)]

    for away in (0, 1, 3, 2):
        handed_over(away).wait_recv()
        z = (layer + LAYERS - away) % LAYERS
        span_live = live[z] > 0.5
        for half in range(2):
            eight = pl.ds(half * 8, 8)
            asked = query[z, eight].reshape(128, HD)
            old_values = old[z, eight, :, HD:WIDTH].reshape(128, HD)
            span_keys = arrived[z, eight, :, 0:HD].reshape(128, HD)
            span_values = arrived[z, eight, :, HD:WIDTH].reshape(128, HD)
            fresh_values = new_values[pl.ds(pl.multiple_of(z * 64 + half * 32, 32), 32), :]
            cached, fresh = score_old[2 * z + half], score_new[2 * z + half]
            may = same & span_live[:, half * 128:half * 128 + 128]
            span = jnp.where(may, dot(asked, span_keys, NT) * scale, -1e30)
            top = jnp.max(jnp.maximum(cached, span), axis=1, keepdims=True)
            top = jnp.maximum(top, jnp.max(fresh, axis=1, keepdims=True))
            cached, span, fresh = jnp.exp(cached - top), jnp.exp(span - top), jnp.exp(fresh - top)
            weight_sum = jnp.sum(cached + span, axis=1, keepdims=True) + jnp.sum(fresh, axis=1, keepdims=True)
            inverse = 1.0 / weight_sum
            result = dot((cached * inverse).astype(BF16), old_values)
            result = result + dot((span * inverse).astype(BF16), span_values)
            result = result + dot((fresh * inverse).astype(BF16), fresh_values)
            out_ref[eight, pl.ds(z, 1)] = result.astype(BF16).reshape(8, 1, SLOT, HD)

    for place in range(CHIPS):
        pair_copy(place).wait_send()
        for h in range(2):
            @pl.when(chip != place)
            def _(place=place, h=h):
                line_copy(0, place, h, partner).wait_send()
    for i in range(1, TP):
        square_copy(i).wait_send()
    for away in (0, 1, 3, 2):
        handed_over(away).wait_send()


def shards(tokens, gain, kv_weight, kv_bias, lengths, dest, queries, old_cache, new_kv):
    query_rows = queries.reshape(GRP, STEPS, QPK, HD).transpose(0, 2, 1, 3).reshape(PLANE, LAYERS, SLOT, HD)
    new_rows = new_kv.reshape(GRP, STEPS, 2, HD).transpose(0, 2, 1, 3).reshape(4 * GRP, HD)
    vmem = pl.BlockSpec(memory_space=pltpu.VMEM)
    dma = pltpu.SemaphoreType.DMA
    out = pl.pallas_call(
        kernel,
        out_shape=jax.ShapeDtypeStruct((PLANE, LAYERS, SLOT, HD), BF16),
        in_specs=[pl.BlockSpec(memory_space=pltpu.HBM)] * 10,
        out_specs=vmem,
        scratch_shapes=[
            pltpu.VMEM((ROWS, FEATS), BF16),
            pltpu.VMEM((ROWS, FEATS), BF16),
            pltpu.VMEM((TP, FEATS, WIDTH), BF16),
            pltpu.VMEM((FEATS,), F32),
            pltpu.VMEM((WIDTH,), F32),
            pltpu.VMEM((GRP, GRP), jnp.int32),
            pltpu.VMEM((GRP, GRP), jnp.int32),
            pltpu.VMEM((LAYERS, PLANE, SLOT, HD), BF16),
            pltpu.VMEM((LAYERS, PLANE, SLOT, WIDTH), BF16),
            pltpu.VMEM((4 * GRP, HD), BF16),
            pltpu.VMEM((4 * GRP, HD), BF16),
            pltpu.VMEM((4 * GRP, HD), BF16),
            pltpu.VMEM((SLOT, 2 * HD), F32),
            pltpu.VMEM((CHIPS, ROWS, WIDTH), BF16),
            pltpu.VMEM((CHIPS, ROWS, WIDTH), BF16),
            pltpu.VMEM((CHIPS, ROWS, WIDTH), F32),
            pltpu.VMEM((2, CHIPS, ROWS, WIDTH), BF16),
            pltpu.VMEM((CHIPS, ROWS, WIDTH), BF16),
            pltpu.VMEM((ROWS, WIDTH), F32),
            pltpu.VMEM((ROWS, WIDTH), BF16),
            pltpu.VMEM((TP, 1, ROWS), F32),
            pltpu.VMEM((LAYERS, LANES, ROWS), BF16),
            pltpu.VMEM((ROWS, HD), F32),
            pltpu.VMEM((ROWS, HD), F32),
            pltpu.VMEM((ROWS, HD), F32),
            pltpu.VMEM((LAYERS, 1, LANES), F32),
            pltpu.VMEM((8, 128, 128), F32),
            pltpu.VMEM((8, 128, 32), F32),
            pltpu.VMEM((LAYERS, PLANE, SLOT, WIDTH), BF16),
            pltpu.VMEM((LAYERS, PLANE, SLOT, WIDTH), BF16),
            pltpu.SemaphoreType.REGULAR,
            pltpu.SemaphoreType.REGULAR,
            dma((15,)),
            dma((TP,)),
            dma((TP,)),
            dma((TP,)),
            dma((CHIPS,)),
            dma((CHIPS,)),
            dma((CHIPS, 2)),
            dma((2, CHIPS, 2)),
            dma((LAYERS,)),
            dma((LAYERS,)),
        ],
        compiler_params=pltpu.CompilerParams(
            collective_id=0, has_side_effects=True, vmem_limit_bytes=40 * 1024 * 1024
        ),
        cost_estimate=pl.CostEstimate(flops=2_500_000_000, bytes_accessed=6_000_000, transcendentals=300_000),
    )(
        *(
            pltpu.with_memory_space_constraint(operand, pltpu.HBM)
            for operand in (
                tokens, kv_weight, gain, kv_bias, lengths, dest,
                query_rows, old_cache.reshape(PLANE, LAYERS, SLOT, WIDTH), new_rows, jnp.asarray(rotary_tables()),
            )
        )
    )
    return out.reshape(GRP, QPK, STEPS, HD).transpose(0, 2, 1, 3).reshape(1, GRP, STEPS, QPK * HD)


def solution(mesh):
    return jax.shard_map(
        shards,
        mesh=mesh,
        in_specs=(
            P("grp", "tp"),
            P("tp"),
            P("tp", None),
            P("tp"),
            P(),
            P(),
            P("grp", None, None, "tp"),
            P("grp", None, None, "tp"),
            P("grp", None, None, "tp"),
        ),
        out_specs=P("grp", None, None, "tp"),
        check_vma=False,
    )
```

```python
import functools
import math

import jax
import jax.numpy as jnp
import numpy as np
from jax import lax
from jax.experimental import pallas as pl
from jax.experimental.pallas import tpu as pltpu
from jax.sharding import PartitionSpec as P

D = 6144
HD = 128
SLOT = 16
CACHED = 16
STEPS = 2
KVW = 2048
QPK = 8
EPSILON = 1e-06
THETA = 1000000.0

ROWS = 512
FEATS = 768
GRP = 64
TP = 8
CHIPS = 4
WIDTH = 256
HALF = ROWS // 2
SLOTS = GRP * SLOT
LAYERS = 4
PLANE = GRP // LAYERS
LANES = PLANE * SLOT
LEADER = 7
CHUNKS = 4
PIECES = 2
LAG = 0.4
PIECE = ROWS // PIECES
MESH = pl.DeviceIdType.MESH
F32 = jnp.float32
BF16 = jnp.bfloat16
NT = (((1,), (1,)), ((), ()))
NN = (((1,), (0,)), ((), ()))


def dot(a, b, dims=NN):
    return lax.dot_general(a, b, dims, preferred_element_type=F32)


def iota(shape, axis):
    return lax.broadcasted_iota(jnp.int32, shape, axis)


def rotary_tables():
    half = HD // 2
    frequency = np.power(np.float32(THETA), -2.0 * np.arange(half, dtype=np.float32) / np.float32(HD)).astype(np.float32)
    angles = ((CACHED + np.arange(SLOT)).astype(np.float32)[:, None] * frequency[None, :]).astype(np.float32)
    cosine, sine = np.cos(angles), np.sin(angles)
    return np.concatenate([cosine, cosine, -sine, sine], axis=1).astype(np.float32)


def kernel(
    tokens_hbm, weight_hbm, gain_hbm, bias_hbm, lengths_hbm, dest_hbm, query_hbm, old_hbm, new_hbm, table_hbm,
    out_ref,
    tokens, scaled, weight, gain_ref, bias_ref, lengths_ref, dest_ref, query, old, new_ref, new_keys, new_values, table_ref,
    pair_out, pair_in, own, landing, line_out, final, handed,
    squares, pick, cos_rows, sin_rows, inverse_rms, live, score_old, score_new, outgoing, arrived,
    joined, all_in,
    load_sem, weight_sem, sq_send, sq_recv, pair_send, pair_recv, line_send, line_recv, hand_send, hand_recv,
):
    group = lax.axis_index("grp")
    tp = lax.axis_index("tp")
    chip = tp // 2
    core = tp % 2
    partner = tp + 1 - 2 * core
    plane, layer = group // LAYERS, group % LAYERS

    load_gain = pltpu.make_async_copy(gain_hbm, gain_ref, load_sem.at[0])
    load_tokens = pltpu.make_async_copy(tokens_hbm, tokens, load_sem.at[1])
    load_gain.start()
    load_tokens.start()

    def head_of(step, whose):
        place = jnp.where(chip < 2, CHIPS - 1 - step, step)
        return place, 2 * place + whose

    def load_weight(chunk):
        rows = pl.ds(chunk * (FEATS // CHUNKS), FEATS // CHUNKS)
        return pltpu.make_async_copy(weight_hbm.at[rows], weight.at[rows], weight_sem.at[chunk])

    def head_weight(head):
        return weight[:, pl.ds(pl.multiple_of(head * WIDTH, WIDTH), WIDTH)]

    for chunk in range(CHUNKS):
        load_weight(chunk).start()
    later_loads = [
        (lengths_hbm, lengths_ref), (dest_hbm, dest_ref), (table_hbm, table_ref), (bias_hbm, bias_ref), (new_hbm, new_ref),
    ]
    for z in range(LAYERS):
        later_loads.append((query_hbm.at[:, z], query.at[z]))
        later_loads.append((old_hbm.at[:, z], old.at[z]))
    later_loads = [
        pltpu.make_async_copy(source, target, load_sem.at[2 + i]) for i, (source, target) in enumerate(later_loads)
    ]

    barrier = pltpu.get_barrier_semaphore()

    def greet_tp(i, carry):
        peer = (tp + i) % TP

        @pl.when(peer != LEADER)
        def _():
            pl.semaphore_signal(barrier, inc=1, device_id={"tp": peer}, device_id_type=MESH)

        return carry

    def greet_leaders(i, carry):
        pl.semaphore_signal(barrier, inc=1, device_id={"grp": (group + i) % GRP}, device_id_type=MESH)
        return carry

    def tell_group(i, carry):
        pl.semaphore_signal(all_in, inc=1, device_id={"tp": (tp + i) % TP}, device_id_type=MESH)
        return carry

    lax.fori_loop(1, TP, greet_tp, 0)

    load_gain.wait()
    load_tokens.wait()
    for h in range(2):
        rows = pl.ds(h * HALF, HALF)
        scaled[rows, :] = (tokens[rows, :].astype(F32) * gain_ref[...][None, :]).astype(BF16)

    @pl.when(tp != LEADER)
    def _():
        pl.semaphore_wait(barrier, TP - 1)
        pl.semaphore_signal(joined, inc=1, device_id={"tp": LEADER}, device_id_type=MESH)

    def pair_copy(place):
        return pltpu.make_async_remote_copy(
            src_ref=pair_out.at[place], dst_ref=pair_in.at[place],
            send_sem=pair_send.at[place], recv_sem=pair_recv.at[place],
            device_id={"tp": partner}, device_id_type=MESH,
        )

    def line_copy(way, place, h, to):
        rows = pl.ds(h * PIECE, PIECE)
        return pltpu.make_async_remote_copy(
            src_ref=line_out.at[place, rows], dst_ref=landing.at[way, place, rows],
            send_sem=line_send.at[place, h], recv_sem=line_recv.at[way, place, h],
            device_id={"tp": to}, device_id_type=MESH,
        )

    def block(place, h):
        rows = pl.ds(h * PIECE, PIECE)
        return own[place, rows] + pair_in[place, rows].astype(F32)

    def multiply_pair(step):
        place, head = head_of(step, 1 - core)
        pair_out[pl.ds(place, 1)] = dot(scaled[...], head_weight(head)).astype(BF16)[None]
        if step == 0:
            @pl.when(tp == LEADER)
            def _():
                pl.semaphore_wait(joined, TP - 1)
                lax.fori_loop(1, GRP, greet_leaders, 0)
        pair_copy(place).start()

    def multiply_own(step):
        place, head = head_of(step, core)
        own[pl.ds(place, 1)] = dot(scaled[...], head_weight(head))[None]

    def first_sends(step):
        place, _ = head_of(step, 0)
        way = chip // (CHIPS - 1)

        @pl.when(chip % (CHIPS - 1) == 0)
        def _():
            pair_copy(place).wait_recv()
            for h in range(PIECES):
                rows = pl.ds(h * PIECE, PIECE)
                line_out[place, rows] = block(place, h).astype(BF16)
                line_copy(way, place, h, tp + 2 - 4 * way).start()

    for load in later_loads:
        load.start()

    def square_copy(i):
        return pltpu.make_async_remote_copy(
            src_ref=squares.at[tp], dst_ref=squares.at[tp],
            send_sem=sq_send.at[i], recv_sem=sq_recv.at[tp],
            device_id={"tp": (tp + i) % TP}, device_id_type=MESH,
        )

    def square_arrival(i):
        source = (tp + i) % TP
        return pltpu.make_async_remote_copy(
            src_ref=squares.at[source], dst_ref=squares.at[source],
            send_sem=sq_send.at[i], recv_sem=sq_recv.at[source],
            device_id={"tp": source}, device_id_type=MESH,
        )

    for chunk in range(CHUNKS):
        load_weight(chunk).wait()
    multiply_pair(0)
    multiply_own(0)
    first_sends(0)
    multiply_pair(1)
    for h in range(2):
        floats = tokens[pl.ds(h * HALF, HALF), :].astype(F32)
        square = floats * floats
        high = square.astype(BF16)
        low = (square - high.astype(F32)).astype(BF16)
        ones = jnp.ones((8, FEATS), BF16)
        sums = dot(ones, high, NT) + dot(ones, low, NT)
        squares[pl.ds(tp, 1), :, h * HALF:(h + 1) * HALF] = sums[0:1, :].reshape(1, 1, HALF)
    for i in range(1, TP):
        square_copy(i).start()
    multiply_pair(2)
    multiply_own(1)
    first_sends(1)
    multiply_pair(3)
    multiply_own(2)
    first_sends(2)
    multiply_own(3)

    for load in later_loads:
        load.wait()
    lengths = lengths_ref[...]
    dests = dest_ref[...]
    mine = iota((GRP, GRP), 0) == group
    own_lengths = jnp.sum(jnp.where(mine, lengths, 0), axis=0, keepdims=True)
    own_dest = jnp.sum(jnp.where(mine, dests, 0), axis=0, keepdims=True)
    before = (iota((GRP, GRP), 0) < iota((GRP, GRP), 1)).astype(F32)
    spread = jnp.broadcast_to(own_lengths.astype(F32), (8, GRP))
    starts = dot(spread, before)[0:1, :].astype(jnp.int32)
    by_layer = iota((GRP, GRP), 0) % PLANE * LAYERS + iota((GRP, GRP), 0) // PLANE
    routed = own_dest == by_layer
    slot_first = jnp.sum(jnp.where(routed, starts, 0), axis=1, keepdims=True)
    slot_length = jnp.sum(jnp.where(routed, own_lengths, 0), axis=1, keepdims=True)
    for part in range(8):
        requests = slice(part * 8, part * 8 + 8)
        offset = iota((8, SLOT, ROWS), 1)
        first = slot_first[requests][:, :, None]
        length = slot_length[requests][:, :, None]
        hit = (iota((8, SLOT, ROWS), 2) == first + offset) & (offset < length)
        pick[part // 2, part % 2 * 128:part % 2 * 128 + 128, :] = hit.astype(F32).reshape(128, ROWS).astype(BF16)

    row_index = iota((ROWS, GRP), 0)
    first_row = jnp.max(jnp.where(starts <= row_index, starts, 0), axis=1, keepdims=True)
    at_offset = (iota((ROWS, SLOT), 1) + first_row == iota((ROWS, SLOT), 0)).astype(F32).astype(BF16)
    rest = table_ref[...]
    tabled = jnp.zeros((ROWS, 2 * HD), F32)
    for _ in range(3):
        term = rest.astype(BF16)
        rest = rest - term.astype(F32)
        tabled = tabled + dot(at_offset, term)
    cos_rows[...] = tabled[:, 0:HD]
    sin_rows[...] = tabled[:, HD:2 * HD]

    live_rows = jnp.sum(jnp.where(dests == group, lengths, 0), axis=1, keepdims=True)
    for z in range(LAYERS):
        at_source = iota((GRP, LANES), 1) // SLOT * LAYERS + z == iota((GRP, LANES), 0)
        live_lanes = jnp.sum(jnp.where(at_source, live_rows, 0), axis=0, keepdims=True)
        live[z] = (iota((1, LANES), 1) % SLOT < live_lanes).astype(F32)

    sorted_row = iota((4 * GRP, 4 * GRP), 0)
    natural = (sorted_row // 4 % PLANE * LAYERS + sorted_row // (4 * PLANE)) * 4 + sorted_row % 4
    column = iota((4 * GRP, 4 * GRP), 1)
    new_keys[...] = dot((column == natural).astype(F32).astype(BF16), new_ref[...]).astype(BF16)
    shifted = (column == natural + 2) & (sorted_row % 4 < 2)
    new_values[...] = dot(shifted.astype(F32).astype(BF16), new_ref[...]).astype(BF16)

    scale = 1.0 / math.sqrt(HD)
    same = iota((128, 128), 0) // 16 == iota((128, 128), 1) // 16
    same_new = (iota((128, 32), 0) // 16 == iota((128, 32), 1) // 4) & (iota((128, 32), 1) % 4 <= iota((128, 32), 0) % 2)
    for z in range(LAYERS):
        for half in range(2):
            eight = slice(half * 8, half * 8 + 8)
            asked = query[z, eight].reshape(128, HD)
            cached_keys = old[z, eight, :, 0:HD].reshape(128, HD)
            fresh_keys = new_keys[z * 64 + half * 32:z * 64 + half * 32 + 32, :]
            score_old[2 * z + half] = jnp.where(same, dot(asked, cached_keys, NT) * scale, -1e30)
            score_new[2 * z + half] = jnp.where(same_new, dot(asked, fresh_keys, NT) * scale, -1e30)

    def schedule(here):
        events = []
        for way in range(2):
            from_end = here if way == 0 else CHIPS - 1 - here
            for back in range(CHIPS - 1):
                place = CHIPS - 1 - back if way == 0 else back
                if from_end and (place >= here if way == 0 else place <= here):
                    for h in range(PIECES):
                        sent = back * PIECES + h + 1
                        events.append((sent + from_end * LAG + (from_end - 1), way, place, h))
        return [event[1:] for event in sorted(events)]

    schedules = {here: schedule(here) for here in range(CHIPS)}
    have = {0: {3, 2, 1}, 1: set(), 2: set(), 3: {0, 1, 2}}
    begun = {here: set() for here in range(CHIPS)}

    def follow(here, events):
        for way, place, h in events:
            if place not in have[here]:
                have[here].add(place)
                pair_copy(place).wait_recv()
            rows = pl.ds(h * PIECE, PIECE)
            value = final[rows, :] if place == here and h in begun[here] else block(place, h)
            line_copy(way, place, h, tp + 4 * way - 2).wait_recv()
            value = value + landing[way, place, rows].astype(F32)
            if place == here:
                begun[here].add(h)
                final[rows, :] = value
            else:
                line_out[place, rows] = value.astype(BF16)
                line_copy(way, place, h, tp + 2 - 4 * way).start()

    def finish(rows):
        inverse = inverse_rms[rows, :]
        keys = final[rows, 0:HD] * inverse + bias_ref[0:HD][None, :]
        values = final[rows, HD:WIDTH] * inverse + bias_ref[HD:WIDTH][None, :]
        turned = pltpu.roll(keys, HD // 2, 1)
        handed[rows, 0:HD] = (keys * cos_rows[rows, :] + turned * sin_rows[rows, :]).astype(BF16)
        handed[rows, HD:WIDTH] = values.astype(BF16)

    @pl.when(tp == LEADER)
    def _():
        pl.semaphore_wait(barrier, GRP - 1)
        lax.fori_loop(1, TP, tell_group, 0)

    for here in range(CHIPS):
        pl.when(chip == here)(functools.partial(follow, here, schedules[here][:-1]))
    for i in range(1, TP):
        square_arrival(i).wait_recv()
    total = jnp.sum(squares[...].reshape(TP, ROWS), axis=0, keepdims=True)
    inverse_rms[...] = jnp.broadcast_to(lax.rsqrt(total / D + EPSILON), (HD, ROWS)).T
    finish(pl.ds(0, ROWS - PIECE))

    @pl.when(tp != LEADER)
    def _():
        pl.semaphore_wait(all_in, 1)

    for here in range(CHIPS):
        pl.when(chip == here)(functools.partial(follow, here, schedules[here][-1:]))
    finish(pl.ds(ROWS - PIECE, PIECE))

    y, x = plane // 4, plane % 4

    def send(aways):
        def body(i, carry):
            target = (y + i // 4) % 4 * 4 + (x + i % 4) % 4
            for away in aways:
                target_layer = (layer + away) % LAYERS
                copy = pltpu.make_async_remote_copy(
                    src_ref=outgoing.at[target_layer, target], dst_ref=arrived.at[layer, plane],
                    send_sem=hand_send.at[away], recv_sem=hand_recv.at[away],
                    device_id={"grp": target * LAYERS + target_layer}, device_id_type=MESH,
                )
                if away:
                    copy.start()
                else:
                    pl.when(i > 0)(copy.start)
            return carry
        return body

    def handed_over(away):
        blocks = pl.ds(0, PLANE if away else PLANE - 1)
        return pltpu.make_async_remote_copy(
            src_ref=outgoing.at[0, blocks], dst_ref=arrived.at[0, blocks],
            send_sem=hand_send.at[away], recv_sem=hand_recv.at[away],
            device_id={"grp": (group + 1) % GRP}, device_id_type=MESH,
        )

    for aways in ((1, 3), (2,), (0,)):
        for away in aways:
            target_layer = (layer + away) % LAYERS
            picked = dot(pick[target_layer], handed[...]).astype(BF16)
            outgoing[pl.ds(target_layer, 1)] = picked.reshape(1, PLANE, SLOT, WIDTH)
        lax.fori_loop(0, PLANE, send(aways), 0)
    arrived[pl.ds(layer, 1), pl.ds(plane, 1)] = outgoing[pl.ds(layer, 1), pl.ds(plane, 1)]

    for away in (0, 1, 3, 2):
        handed_over(away).wait_recv()
        z = (layer + LAYERS - away) % LAYERS
        span_live = live[z] > 0.5
        for half in range(2):
            eight = pl.ds(half * 8, 8)
            asked = query[z, eight].reshape(128, HD)
            old_values = old[z, eight, :, HD:WIDTH].reshape(128, HD)
            span_keys = arrived[z, eight, :, 0:HD].reshape(128, HD)
            span_values = arrived[z, eight, :, HD:WIDTH].reshape(128, HD)
            fresh_values = new_values[pl.ds(pl.multiple_of(z * 64 + half * 32, 32), 32), :]
            cached, fresh = score_old[2 * z + half], score_new[2 * z + half]
            may = same & span_live[:, half * 128:half * 128 + 128]
            span = jnp.where(may, dot(asked, span_keys, NT) * scale, -1e30)
            top = jnp.max(jnp.maximum(cached, span), axis=1, keepdims=True)
            top = jnp.maximum(top, jnp.max(fresh, axis=1, keepdims=True))
            cached, span, fresh = jnp.exp(cached - top), jnp.exp(span - top), jnp.exp(fresh - top)
            weight_sum = jnp.sum(cached + span, axis=1, keepdims=True) + jnp.sum(fresh, axis=1, keepdims=True)
            inverse = 1.0 / weight_sum
            result = dot((cached * inverse).astype(BF16), old_values)
            result = result + dot((span * inverse).astype(BF16), span_values)
            result = result + dot((fresh * inverse).astype(BF16), fresh_values)
            out_ref[eight, pl.ds(z, 1)] = result.astype(BF16).reshape(8, 1, SLOT, HD)

    for place in range(CHIPS):
        pair_copy(place).wait_send()
        for h in range(PIECES):
            @pl.when(chip != place)
            def _(place=place, h=h):
                line_copy(0, place, h, partner).wait_send()
    for i in range(1, TP):
        square_copy(i).wait_send()
    for away in (0, 1, 3, 2):
        handed_over(away).wait_send()


def shards(tokens, gain, kv_weight, kv_bias, lengths, dest, queries, old_cache, new_kv):
    query_rows = queries.reshape(GRP, STEPS, QPK, HD).transpose(0, 2, 1, 3).reshape(PLANE, LAYERS, SLOT, HD)
    new_rows = new_kv.reshape(GRP, STEPS, 2, HD).transpose(0, 2, 1, 3).reshape(4 * GRP, HD)
    vmem = pl.BlockSpec(memory_space=pltpu.VMEM)
    dma = pltpu.SemaphoreType.DMA
    out = pl.pallas_call(
        kernel,
        out_shape=jax.ShapeDtypeStruct((PLANE, LAYERS, SLOT, HD), BF16),
        in_specs=[pl.BlockSpec(memory_space=pltpu.HBM)] * 10,
        out_specs=vmem,
        scratch_shapes=[
            pltpu.VMEM((ROWS, FEATS), BF16),
            pltpu.VMEM((ROWS, FEATS), BF16),
            pltpu.VMEM((FEATS, KVW), BF16),
            pltpu.VMEM((FEATS,), F32),
            pltpu.VMEM((WIDTH,), F32),
            pltpu.VMEM((GRP, GRP), jnp.int32),
            pltpu.VMEM((GRP, GRP), jnp.int32),
            pltpu.VMEM((LAYERS, PLANE, SLOT, HD), BF16),
            pltpu.VMEM((LAYERS, PLANE, SLOT, WIDTH), BF16),
            pltpu.VMEM((4 * GRP, HD), BF16),
            pltpu.VMEM((4 * GRP, HD), BF16),
            pltpu.VMEM((4 * GRP, HD), BF16),
            pltpu.VMEM((SLOT, 2 * HD), F32),
            pltpu.VMEM((CHIPS, ROWS, WIDTH), BF16),
            pltpu.VMEM((CHIPS, ROWS, WIDTH), BF16),
            pltpu.VMEM((CHIPS, ROWS, WIDTH), F32),
            pltpu.VMEM((2, CHIPS, ROWS, WIDTH), BF16),
            pltpu.VMEM((CHIPS, ROWS, WIDTH), BF16),
            pltpu.VMEM((ROWS, WIDTH), F32),
            pltpu.VMEM((ROWS, WIDTH), BF16),
            pltpu.VMEM((TP, 1, ROWS), F32),
            pltpu.VMEM((LAYERS, LANES, ROWS), BF16),
            pltpu.VMEM((ROWS, HD), F32),
            pltpu.VMEM((ROWS, HD), F32),
            pltpu.VMEM((ROWS, HD), F32),
            pltpu.VMEM((LAYERS, 1, LANES), F32),
            pltpu.VMEM((8, 128, 128), F32),
            pltpu.VMEM((8, 128, 32), F32),
            pltpu.VMEM((LAYERS, PLANE, SLOT, WIDTH), BF16),
            pltpu.VMEM((LAYERS, PLANE, SLOT, WIDTH), BF16),
            pltpu.SemaphoreType.REGULAR,
            pltpu.SemaphoreType.REGULAR,
            dma((15,)),
            dma((CHUNKS,)),
            dma((TP,)),
            dma((TP,)),
            dma((CHIPS,)),
            dma((CHIPS,)),
            dma((CHIPS, PIECES)),
            dma((2, CHIPS, PIECES)),
            dma((LAYERS,)),
            dma((LAYERS,)),
        ],
        compiler_params=pltpu.CompilerParams(
            collective_id=0, has_side_effects=True, vmem_limit_bytes=40 * 1024 * 1024
        ),
        cost_estimate=pl.CostEstimate(flops=2_500_000_000, bytes_accessed=6_000_000, transcendentals=300_000),
    )(
        *(
            pltpu.with_memory_space_constraint(operand, pltpu.HBM)
            for operand in (
                tokens, kv_weight, gain, kv_bias, lengths, dest,
                query_rows, old_cache.reshape(PLANE, LAYERS, SLOT, WIDTH), new_rows, jnp.asarray(rotary_tables()),
            )
        )
    )
    return out.reshape(GRP, QPK, STEPS, HD).transpose(0, 2, 1, 3).reshape(1, GRP, STEPS, QPK * HD)


def solution(mesh):
    return jax.shard_map(
        shards,
        mesh=mesh,
        in_specs=(
            P("grp", "tp"),
            P("tp"),
            P("tp", None),
            P("tp"),
            P(),
            P(),
            P("grp", None, None, "tp"),
            P("grp", None, None, "tp"),
            P("grp", None, None, "tp"),
        ),
        out_specs=P("grp", None, None, "tp"),
        check_vma=False,
    )
```

```python
import functools
import math

import jax
import jax.numpy as jnp
import numpy as np
from jax import lax
from jax.experimental import pallas as pl
from jax.experimental.pallas import tpu as pltpu
from jax.sharding import PartitionSpec as P

D = 6144
HD = 128
SLOT = 16
CACHED = 16
STEPS = 2
KVW = 2048
QPK = 8
EPSILON = 1e-06
THETA = 1000000.0

ROWS = 512
FEATS = 768
GRP = 64
TP = 8
CHIPS = 4
WIDTH = 256
HALF = ROWS // 2
SLOTS = GRP * SLOT
LAYERS = 4
PLANE = GRP // LAYERS
LANES = PLANE * SLOT
LEADER = 7
CHUNKS = 3
PIECES = 2
LAG = 0.4
PIECE = ROWS // PIECES
MESH = pl.DeviceIdType.MESH
F32 = jnp.float32
BF16 = jnp.bfloat16
NT = (((1,), (1,)), ((), ()))
NN = (((1,), (0,)), ((), ()))


def dot(a, b, dims=NN):
    return lax.dot_general(a, b, dims, preferred_element_type=F32)


def iota(shape, axis):
    return lax.broadcasted_iota(jnp.int32, shape, axis)


def rotary_tables():
    half = HD // 2
    frequency = np.power(np.float32(THETA), -2.0 * np.arange(half, dtype=np.float32) / np.float32(HD)).astype(np.float32)
    angles = ((CACHED + np.arange(SLOT)).astype(np.float32)[:, None] * frequency[None, :]).astype(np.float32)
    cosine, sine = np.cos(angles), np.sin(angles)
    return np.concatenate([cosine, cosine, -sine, sine], axis=1).astype(np.float32)


def kernel(
    tokens_hbm, weight_hbm, gain_hbm, bias_hbm, lengths_hbm, dest_hbm, query_hbm, old_hbm, new_hbm, table_hbm,
    out_ref,
    tokens, scaled, weight, gain_ref, bias_ref, lengths_ref, dest_ref, query, old, new_ref, new_keys, new_values, table_ref,
    pair_out, pair_in, own, landing, line_out, final, handed, early,
    squares, pick, cos_rows, sin_rows, inverse_rms, live, score_old, score_new, outgoing, arrived,
    joined, all_in,
    load_sem, weight_sem, sq_send, sq_recv, pair_send, pair_recv, line_send, line_recv, hand_send, hand_recv,
):
    group = lax.axis_index("grp")
    tp = lax.axis_index("tp")
    chip = tp // 2
    core = tp % 2
    partner = tp + 1 - 2 * core
    plane, layer = group // LAYERS, group % LAYERS

    load_gain = pltpu.make_async_copy(gain_hbm, gain_ref, load_sem.at[0])
    load_tokens = pltpu.make_async_copy(tokens_hbm, tokens, load_sem.at[1])
    load_gain.start()
    load_tokens.start()

    def head_of(step, whose):
        place = jnp.where(chip < 2, CHIPS - 1 - step, step)
        return place, 2 * place + whose

    def load_weight(chunk):
        rows = pl.ds(chunk * (FEATS // CHUNKS), FEATS // CHUNKS)
        return pltpu.make_async_copy(weight_hbm.at[rows], weight.at[rows], weight_sem.at[chunk])

    def head_weight(head):
        return weight[:, pl.ds(pl.multiple_of(head * WIDTH, WIDTH), WIDTH)]

    for chunk in range(CHUNKS):
        load_weight(chunk).start()
    later_loads = [
        (lengths_hbm, lengths_ref), (dest_hbm, dest_ref), (table_hbm, table_ref), (bias_hbm, bias_ref), (new_hbm, new_ref),
    ]
    for z in range(LAYERS):
        later_loads.append((query_hbm.at[:, z], query.at[z]))
        later_loads.append((old_hbm.at[:, z], old.at[z]))
    later_loads = [
        pltpu.make_async_copy(source, target, load_sem.at[2 + i]) for i, (source, target) in enumerate(later_loads)
    ]

    barrier = pltpu.get_barrier_semaphore()

    def greet_tp(i, carry):
        peer = (tp + i) % TP

        @pl.when(peer != LEADER)
        def _():
            pl.semaphore_signal(barrier, inc=1, device_id={"tp": peer}, device_id_type=MESH)

        return carry

    def greet_leaders(i, carry):
        pl.semaphore_signal(barrier, inc=1, device_id={"grp": (group + i) % GRP}, device_id_type=MESH)
        return carry

    def tell_group(i, carry):
        pl.semaphore_signal(all_in, inc=1, device_id={"tp": (tp + i) % TP}, device_id_type=MESH)
        return carry

    lax.fori_loop(1, TP, greet_tp, 0)

    load_gain.wait()
    load_tokens.wait()
    for h in range(2):
        rows = pl.ds(h * HALF, HALF)
        scaled[rows, :] = (tokens[rows, :].astype(F32) * gain_ref[...][None, :]).astype(BF16)

    @pl.when(tp != LEADER)
    def _():
        pl.semaphore_wait(barrier, TP - 1)
        pl.semaphore_signal(joined, inc=1, device_id={"tp": LEADER}, device_id_type=MESH)

    def pair_copy(place):
        return pltpu.make_async_remote_copy(
            src_ref=pair_out.at[place], dst_ref=pair_in.at[place],
            send_sem=pair_send.at[place], recv_sem=pair_recv.at[place],
            device_id={"tp": partner}, device_id_type=MESH,
        )

    def line_copy(way, place, h, to):
        rows = pl.ds(h * PIECE, PIECE)
        return pltpu.make_async_remote_copy(
            src_ref=line_out.at[place, rows], dst_ref=landing.at[way, place, rows],
            send_sem=line_send.at[place, h], recv_sem=line_recv.at[way, place, h],
            device_id={"tp": to}, device_id_type=MESH,
        )

    def block(place, h):
        rows = pl.ds(h * PIECE, PIECE)
        return own[place, rows] + pair_in[place, rows].astype(F32)

    def multiply_pair(step):
        place, head = head_of(step, 1 - core)
        pair_out[pl.ds(place, 1)] = dot(scaled[...], head_weight(head)).astype(BF16)[None]
        pair_copy(place).start()

    def multiply_first():
        place, pair_head = head_of(0, 1 - core)
        _, own_head = head_of(0, core)
        depth = FEATS // CHUNKS
        for chunk in range(CHUNKS):
            load_weight(chunk).wait()
            features = slice(chunk * depth, chunk * depth + depth)
            part = scaled[:, features]
            pair_part = dot(part, weight[features, pl.ds(pl.multiple_of(pair_head * WIDTH, WIDTH), WIDTH)])
            own_part = dot(part, weight[features, pl.ds(pl.multiple_of(own_head * WIDTH, WIDTH), WIDTH)])
            if chunk == 0:
                final[...] = pair_part
                own[pl.ds(place, 1)] = own_part[None]
            elif chunk < CHUNKS - 1:
                final[...] += pair_part
                own[pl.ds(place, 1)] += own_part[None]
            else:
                pair_out[pl.ds(place, 1)] = (final[...] + pair_part).astype(BF16)[None]

                @pl.when(tp == LEADER)
                def _():
                    pl.semaphore_wait(joined, TP - 1)
                    lax.fori_loop(1, GRP, greet_leaders, 0)

                pair_copy(place).start()
                own[pl.ds(place, 1)] += own_part[None]

    def multiply_own(step):
        place, head = head_of(step, core)
        own[pl.ds(place, 1)] = dot(scaled[...], head_weight(head))[None]

    def first_sends(step):
        place, _ = head_of(step, 0)
        way = chip // (CHIPS - 1)

        @pl.when(chip % (CHIPS - 1) == 0)
        def _():
            pair_copy(place).wait_recv()
            for h in range(PIECES):
                rows = pl.ds(h * PIECE, PIECE)
                line_out[place, rows] = block(place, h).astype(BF16)
                line_copy(way, place, h, tp + 2 - 4 * way).start()

    for load in later_loads:
        load.start()

    def square_copy(i):
        return pltpu.make_async_remote_copy(
            src_ref=squares.at[tp], dst_ref=squares.at[tp],
            send_sem=sq_send.at[i], recv_sem=sq_recv.at[tp],
            device_id={"tp": (tp + i) % TP}, device_id_type=MESH,
        )

    def square_arrival(i):
        source = (tp + i) % TP
        return pltpu.make_async_remote_copy(
            src_ref=squares.at[source], dst_ref=squares.at[source],
            send_sem=sq_send.at[i], recv_sem=sq_recv.at[source],
            device_id={"tp": source}, device_id_type=MESH,
        )

    multiply_first()
    first_sends(0)
    multiply_pair(1)
    for h in range(2):
        floats = tokens[pl.ds(h * HALF, HALF), :].astype(F32)
        square = floats * floats
        high = square.astype(BF16)
        low = (square - high.astype(F32)).astype(BF16)
        ones = jnp.ones((8, FEATS), BF16)
        sums = dot(ones, high, NT) + dot(ones, low, NT)
        squares[pl.ds(tp, 1), :, h * HALF:(h + 1) * HALF] = sums[0:1, :].reshape(1, 1, HALF)
    for i in range(1, TP):
        square_copy(i).start()
    multiply_pair(2)
    multiply_own(1)
    first_sends(1)
    multiply_pair(3)
    multiply_own(2)
    first_sends(2)
    multiply_own(3)

    for load in later_loads:
        load.wait()
    lengths = lengths_ref[...]
    dests = dest_ref[...]
    mine = iota((GRP, GRP), 0) == group
    own_lengths = jnp.sum(jnp.where(mine, lengths, 0), axis=0, keepdims=True)
    own_dest = jnp.sum(jnp.where(mine, dests, 0), axis=0, keepdims=True)
    before = (iota((GRP, GRP), 0) < iota((GRP, GRP), 1)).astype(F32)
    spread = jnp.broadcast_to(own_lengths.astype(F32), (8, GRP))
    starts = dot(spread, before)[0:1, :].astype(jnp.int32)
    by_layer = iota((GRP, GRP), 0) % PLANE * LAYERS + iota((GRP, GRP), 0) // PLANE
    routed = own_dest == by_layer
    slot_first = jnp.sum(jnp.where(routed, starts, 0), axis=1, keepdims=True)
    slot_length = jnp.sum(jnp.where(routed, own_lengths, 0), axis=1, keepdims=True)
    for part in range(8):
        requests = slice(part * 8, part * 8 + 8)
        offset = iota((8, SLOT, ROWS), 1)
        first = slot_first[requests][:, :, None]
        length = slot_length[requests][:, :, None]
        hit = (iota((8, SLOT, ROWS), 2) == first + offset) & (offset < length)
        pick[part // 2, part % 2 * 128:part % 2 * 128 + 128, :] = hit.astype(F32).reshape(128, ROWS).astype(BF16)

    row_index = iota((ROWS, GRP), 0)
    first_row = jnp.max(jnp.where(starts <= row_index, starts, 0), axis=1, keepdims=True)
    at_offset = (iota((ROWS, SLOT), 1) + first_row == iota((ROWS, SLOT), 0)).astype(F32).astype(BF16)
    rest = table_ref[...]
    tabled = jnp.zeros((ROWS, 2 * HD), F32)
    for _ in range(3):
        term = rest.astype(BF16)
        rest = rest - term.astype(F32)
        tabled = tabled + dot(at_offset, term)
    cos_rows[...] = tabled[:, 0:HD]
    sin_rows[...] = tabled[:, HD:2 * HD]

    live_rows = jnp.sum(jnp.where(dests == group, lengths, 0), axis=1, keepdims=True)
    for z in range(LAYERS):
        at_source = iota((GRP, LANES), 1) // SLOT * LAYERS + z == iota((GRP, LANES), 0)
        live_lanes = jnp.sum(jnp.where(at_source, live_rows, 0), axis=0, keepdims=True)
        live[z] = (iota((1, LANES), 1) % SLOT < live_lanes).astype(F32)

    sorted_row = iota((4 * GRP, 4 * GRP), 0)
    natural = (sorted_row // 4 % PLANE * LAYERS + sorted_row // (4 * PLANE)) * 4 + sorted_row % 4
    column = iota((4 * GRP, 4 * GRP), 1)
    new_keys[...] = dot((column == natural).astype(F32).astype(BF16), new_ref[...]).astype(BF16)
    shifted = (column == natural + 2) & (sorted_row % 4 < 2)
    new_values[...] = dot(shifted.astype(F32).astype(BF16), new_ref[...]).astype(BF16)

    scale = 1.0 / math.sqrt(HD)
    same = iota((128, 128), 0) // 16 == iota((128, 128), 1) // 16
    same_new = (iota((128, 32), 0) // 16 == iota((128, 32), 1) // 4) & (iota((128, 32), 1) % 4 <= iota((128, 32), 0) % 2)
    for z in range(LAYERS):
        for half in range(2):
            eight = slice(half * 8, half * 8 + 8)
            asked = query[z, eight].reshape(128, HD)
            cached_keys = old[z, eight, :, 0:HD].reshape(128, HD)
            fresh_keys = new_keys[z * 64 + half * 32:z * 64 + half * 32 + 32, :]
            score_old[2 * z + half] = jnp.where(same, dot(asked, cached_keys, NT) * scale, -1e30)
            score_new[2 * z + half] = jnp.where(same_new, dot(asked, fresh_keys, NT) * scale, -1e30)

    def schedule(here):
        events = []
        for way in range(2):
            from_end = here if way == 0 else CHIPS - 1 - here
            for back in range(CHIPS - 1):
                place = CHIPS - 1 - back if way == 0 else back
                if from_end and (place >= here if way == 0 else place <= here):
                    for h in range(PIECES):
                        sent = back * PIECES + h + 1
                        events.append((sent + from_end * LAG + (from_end - 1), way, place, h))
        return [event[1:] for event in sorted(events)]

    schedules = {here: schedule(here) for here in range(CHIPS)}
    have = {0: {3, 2, 1}, 1: set(), 2: set(), 3: {0, 1, 2}}
    begun = {here: set() for here in range(CHIPS)}

    def follow(here, events):
        for way, place, h in events:
            if place not in have[here]:
                have[here].add(place)
                pair_copy(place).wait_recv()
            rows = pl.ds(h * PIECE, PIECE)
            value = final[rows, :] if place == here and h in begun[here] else block(place, h)
            line_copy(way, place, h, tp + 4 * way - 2).wait_recv()
            value = value + landing[way, place, rows].astype(F32)
            if place == here:
                begun[here].add(h)
                final[rows, :] = value
            else:
                line_out[place, rows] = value.astype(BF16)
                line_copy(way, place, h, tp + 2 - 4 * way).start()

    def finish(rows):
        inverse = inverse_rms[rows, :]
        keys = final[rows, 0:HD] * inverse + bias_ref[0:HD][None, :]
        values = final[rows, HD:WIDTH] * inverse + bias_ref[HD:WIDTH][None, :]
        turned = pltpu.roll(keys, HD // 2, 1)
        handed[rows, 0:HD] = (keys * cos_rows[rows, :] + turned * sin_rows[rows, :]).astype(BF16)
        handed[rows, HD:WIDTH] = values.astype(BF16)

    @pl.when(tp == LEADER)
    def _():
        pl.semaphore_wait(barrier, GRP - 1)
        lax.fori_loop(1, TP, tell_group, 0)

    for here in range(CHIPS):
        pl.when(chip == here)(functools.partial(follow, here, schedules[here][:-1]))
    for i in range(1, TP):
        square_arrival(i).wait_recv()
    total = jnp.sum(squares[...].reshape(TP, ROWS), axis=0, keepdims=True)
    inverse_rms[...] = jnp.broadcast_to(lax.rsqrt(total / D + EPSILON), (HD, ROWS)).T
    finish(pl.ds(0, ROWS - PIECE))
    for z in range(LAYERS):
        early[z] = dot(pick[z, :, 0:ROWS - PIECE], handed[0:ROWS - PIECE, :])

    @pl.when(tp != LEADER)
    def _():
        pl.semaphore_wait(all_in, 1)

    for here in range(CHIPS):
        pl.when(chip == here)(functools.partial(follow, here, schedules[here][-1:]))
    finish(pl.ds(ROWS - PIECE, PIECE))

    y, x = plane // 4, plane % 4

    def send(aways):
        def body(i, carry):
            target = (y + i // 4) % 4 * 4 + (x + i % 4) % 4
            for away in aways:
                target_layer = (layer + away) % LAYERS
                copy = pltpu.make_async_remote_copy(
                    src_ref=outgoing.at[target_layer, target], dst_ref=arrived.at[layer, plane],
                    send_sem=hand_send.at[away], recv_sem=hand_recv.at[away],
                    device_id={"grp": target * LAYERS + target_layer}, device_id_type=MESH,
                )
                if away:
                    copy.start()
                else:
                    pl.when(i > 0)(copy.start)
            return carry
        return body

    def handed_over(away):
        blocks = pl.ds(0, PLANE if away else PLANE - 1)
        return pltpu.make_async_remote_copy(
            src_ref=outgoing.at[0, blocks], dst_ref=arrived.at[0, blocks],
            send_sem=hand_send.at[away], recv_sem=hand_recv.at[away],
            device_id={"grp": (group + 1) % GRP}, device_id_type=MESH,
        )

    for aways in ((1, 3), (2,), (0,)):
        for away in aways:
            target_layer = (layer + away) % LAYERS
            late = dot(pick[target_layer, :, ROWS - PIECE:ROWS], handed[ROWS - PIECE:ROWS, :])
            picked = (early[target_layer] + late).astype(BF16)
            outgoing[pl.ds(target_layer, 1)] = picked.reshape(1, PLANE, SLOT, WIDTH)
        lax.fori_loop(0, PLANE, send(aways), 0)
    arrived[pl.ds(layer, 1), pl.ds(plane, 1)] = outgoing[pl.ds(layer, 1), pl.ds(plane, 1)]

    for away in (0, 1, 3, 2):
        handed_over(away).wait_recv()
        z = (layer + LAYERS - away) % LAYERS
        span_live = live[z] > 0.5
        for half in range(2):
            eight = pl.ds(half * 8, 8)
            asked = query[z, eight].reshape(128, HD)
            old_values = old[z, eight, :, HD:WIDTH].reshape(128, HD)
            span_keys = arrived[z, eight, :, 0:HD].reshape(128, HD)
            span_values = arrived[z, eight, :, HD:WIDTH].reshape(128, HD)
            fresh_values = new_values[pl.ds(pl.multiple_of(z * 64 + half * 32, 32), 32), :]
            cached, fresh = score_old[2 * z + half], score_new[2 * z + half]
            may = same & span_live[:, half * 128:half * 128 + 128]
            span = jnp.where(may, dot(asked, span_keys, NT) * scale, -1e30)
            top = jnp.max(jnp.maximum(cached, span), axis=1, keepdims=True)
            top = jnp.maximum(top, jnp.max(fresh, axis=1, keepdims=True))
            cached, span, fresh = jnp.exp(cached - top), jnp.exp(span - top), jnp.exp(fresh - top)
            weight_sum = jnp.sum(cached + span, axis=1, keepdims=True) + jnp.sum(fresh, axis=1, keepdims=True)
            inverse = 1.0 / weight_sum
            result = dot((cached * inverse).astype(BF16), old_values)
            result = result + dot((span * inverse).astype(BF16), span_values)
            result = result + dot((fresh * inverse).astype(BF16), fresh_values)
            out_ref[eight, pl.ds(z, 1)] = result.astype(BF16).reshape(8, 1, SLOT, HD)

    for place in range(CHIPS):
        pair_copy(place).wait_send()
        for h in range(PIECES):
            @pl.when(chip != place)
            def _(place=place, h=h):
                line_copy(0, place, h, partner).wait_send()
    for i in range(1, TP):
        square_copy(i).wait_send()
    for away in (0, 1, 3, 2):
        handed_over(away).wait_send()


def shards(tokens, gain, kv_weight, kv_bias, lengths, dest, queries, old_cache, new_kv):
    query_rows = queries.reshape(GRP, STEPS, QPK, HD).transpose(0, 2, 1, 3).reshape(PLANE, LAYERS, SLOT, HD)
    new_rows = new_kv.reshape(GRP, STEPS, 2, HD).transpose(0, 2, 1, 3).reshape(4 * GRP, HD)
    vmem = pl.BlockSpec(memory_space=pltpu.VMEM)
    dma = pltpu.SemaphoreType.DMA
    out = pl.pallas_call(
        kernel,
        out_shape=jax.ShapeDtypeStruct((PLANE, LAYERS, SLOT, HD), BF16),
        in_specs=[pl.BlockSpec(memory_space=pltpu.HBM)] * 10,
        out_specs=vmem,
        scratch_shapes=[
            pltpu.VMEM((ROWS, FEATS), BF16),
            pltpu.VMEM((ROWS, FEATS), BF16),
            pltpu.VMEM((FEATS, KVW), BF16),
            pltpu.VMEM((FEATS,), F32),
            pltpu.VMEM((WIDTH,), F32),
            pltpu.VMEM((GRP, GRP), jnp.int32),
            pltpu.VMEM((GRP, GRP), jnp.int32),
            pltpu.VMEM((LAYERS, PLANE, SLOT, HD), BF16),
            pltpu.VMEM((LAYERS, PLANE, SLOT, WIDTH), BF16),
            pltpu.VMEM((4 * GRP, HD), BF16),
            pltpu.VMEM((4 * GRP, HD), BF16),
            pltpu.VMEM((4 * GRP, HD), BF16),
            pltpu.VMEM((SLOT, 2 * HD), F32),
            pltpu.VMEM((CHIPS, ROWS, WIDTH), BF16),
            pltpu.VMEM((CHIPS, ROWS, WIDTH), BF16),
            pltpu.VMEM((CHIPS, ROWS, WIDTH), F32),
            pltpu.VMEM((2, CHIPS, ROWS, WIDTH), BF16),
            pltpu.VMEM((CHIPS, ROWS, WIDTH), BF16),
            pltpu.VMEM((ROWS, WIDTH), F32),
            pltpu.VMEM((ROWS, WIDTH), BF16),
            pltpu.VMEM((LAYERS, LANES, WIDTH), F32),
            pltpu.VMEM((TP, 1, ROWS), F32),
            pltpu.VMEM((LAYERS, LANES, ROWS), BF16),
            pltpu.VMEM((ROWS, HD), F32),
            pltpu.VMEM((ROWS, HD), F32),
            pltpu.VMEM((ROWS, HD), F32),
            pltpu.VMEM((LAYERS, 1, LANES), F32),
            pltpu.VMEM((8, 128, 128), F32),
            pltpu.VMEM((8, 128, 32), F32),
            pltpu.VMEM((LAYERS, PLANE, SLOT, WIDTH), BF16),
            pltpu.VMEM((LAYERS, PLANE, SLOT, WIDTH), BF16),
            pltpu.SemaphoreType.REGULAR,
            pltpu.SemaphoreType.REGULAR,
            dma((15,)),
            dma((CHUNKS,)),
            dma((TP,)),
            dma((TP,)),
            dma((CHIPS,)),
            dma((CHIPS,)),
            dma((CHIPS, PIECES)),
            dma((2, CHIPS, PIECES)),
            dma((LAYERS,)),
            dma((LAYERS,)),
        ],
        compiler_params=pltpu.CompilerParams(
            collective_id=0, has_side_effects=True, vmem_limit_bytes=40 * 1024 * 1024
        ),
        cost_estimate=pl.CostEstimate(flops=2_500_000_000, bytes_accessed=6_000_000, transcendentals=300_000),
    )(
        *(
            pltpu.with_memory_space_constraint(operand, pltpu.HBM)
            for operand in (
                tokens, kv_weight, gain, kv_bias, lengths, dest,
                query_rows, old_cache.reshape(PLANE, LAYERS, SLOT, WIDTH), new_rows, jnp.asarray(rotary_tables()),
            )
        )
    )
    return out.reshape(GRP, QPK, STEPS, HD).transpose(0, 2, 1, 3).reshape(1, GRP, STEPS, QPK * HD)


def solution(mesh):
    return jax.shard_map(
        shards,
        mesh=mesh,
        in_specs=(
            P("grp", "tp"),
            P("tp"),
            P("tp", None),
            P("tp"),
            P(),
            P(),
            P("grp", None, None, "tp"),
            P("grp", None, None, "tp"),
            P("grp", None, None, "tp"),
        ),
        out_specs=P("grp", None, None, "tp"),
        check_vma=False,
    )
```

```python
import functools
import math

import jax
import jax.numpy as jnp
import numpy as np
from jax import lax
from jax.experimental import pallas as pl
from jax.experimental.pallas import tpu as pltpu
from jax.sharding import PartitionSpec as P

D = 6144
HD = 128
SLOT = 16
CACHED = 16
STEPS = 2
KVW = 2048
QPK = 8
EPSILON = 1e-06
THETA = 1000000.0

ROWS = 512
FEATS = 768
GRP = 64
TP = 8
CHIPS = 4
WIDTH = 256
HALF = ROWS // 2
SLOTS = GRP * SLOT
LAYERS = 4
PLANE = GRP // LAYERS
LANES = PLANE * SLOT
LEADER = 7
CHUNKS = 4
PIECES = 2
LAG = 0.4
PIECE = ROWS // PIECES
MESH = pl.DeviceIdType.MESH
F32 = jnp.float32
BF16 = jnp.bfloat16
NT = (((1,), (1,)), ((), ()))
NN = (((1,), (0,)), ((), ()))


def dot(a, b, dims=NN):
    return lax.dot_general(a, b, dims, preferred_element_type=F32)


def iota(shape, axis):
    return lax.broadcasted_iota(jnp.int32, shape, axis)


def rotary_tables():
    half = HD // 2
    frequency = np.power(np.float32(THETA), -2.0 * np.arange(half, dtype=np.float32) / np.float32(HD)).astype(np.float32)
    angles = ((CACHED + np.arange(SLOT)).astype(np.float32)[:, None] * frequency[None, :]).astype(np.float32)
    cosine, sine = np.cos(angles), np.sin(angles)
    return np.concatenate([cosine, cosine, -sine, sine], axis=1).astype(np.float32)


def kernel(
    tokens_hbm, weight_hbm, gain_hbm, bias_hbm, lengths_hbm, dest_hbm, query_hbm, old_hbm, new_hbm, table_hbm,
    out_ref,
    tokens, scaled, weight, gain_ref, bias_ref, lengths_ref, dest_ref, query, old, new_ref, new_keys, new_values, table_ref,
    pair_out, pair_in, own, landing, line_out, final, handed, early,
    squares, pick, cos_rows, sin_rows, inverse_rms, live, score_old, score_new, outgoing, arrived,
    joined, all_in,
    load_sem, weight_sem, sq_send, sq_recv, pair_send, pair_recv, line_send, line_recv, hand_send, hand_recv,
):
    group = lax.axis_index("grp")
    tp = lax.axis_index("tp")
    chip = tp // 2
    core = tp % 2
    partner = tp + 1 - 2 * core
    plane, layer = group // LAYERS, group % LAYERS

    load_gain = pltpu.make_async_copy(gain_hbm, gain_ref, load_sem.at[0])
    load_tokens = pltpu.make_async_copy(tokens_hbm, tokens, load_sem.at[1])
    load_gain.start()
    load_tokens.start()

    def head_of(step, whose):
        place = jnp.where(chip < 2, CHIPS - 1 - step, step)
        return place, 2 * place + whose

    def load_weight(chunk):
        rows = pl.ds(chunk * (FEATS // CHUNKS), FEATS // CHUNKS)
        return pltpu.make_async_copy(weight_hbm.at[rows], weight.at[rows], weight_sem.at[chunk])

    def head_weight(head):
        return weight[:, pl.ds(pl.multiple_of(head * WIDTH, WIDTH), WIDTH)]

    for chunk in range(CHUNKS):
        load_weight(chunk).start()
    later_loads = [
        (lengths_hbm, lengths_ref), (dest_hbm, dest_ref), (table_hbm, table_ref), (bias_hbm, bias_ref), (new_hbm, new_ref),
    ]
    for z in range(LAYERS):
        later_loads.append((query_hbm.at[:, z], query.at[z]))
        later_loads.append((old_hbm.at[:, z], old.at[z]))
    later_loads = [
        pltpu.make_async_copy(source, target, load_sem.at[2 + i]) for i, (source, target) in enumerate(later_loads)
    ]

    barrier = pltpu.get_barrier_semaphore()

    def greet_tp(i, carry):
        peer = (tp + i) % TP

        @pl.when(peer != LEADER)
        def _():
            pl.semaphore_signal(barrier, inc=1, device_id={"tp": peer}, device_id_type=MESH)

        return carry

    def greet_leaders(i, carry):
        pl.semaphore_signal(barrier, inc=1, device_id={"grp": (group + i) % GRP}, device_id_type=MESH)
        return carry

    def tell_group(i, carry):
        pl.semaphore_signal(all_in, inc=1, device_id={"tp": (tp + i) % TP}, device_id_type=MESH)
        return carry

    lax.fori_loop(1, TP, greet_tp, 0)

    load_gain.wait()
    load_tokens.wait()
    for h in range(2):
        rows = pl.ds(h * HALF, HALF)
        scaled[rows, :] = (tokens[rows, :].astype(F32) * gain_ref[...][None, :]).astype(BF16)

    @pl.when(tp != LEADER)
    def _():
        pl.semaphore_wait(barrier, TP - 1)
        pl.semaphore_signal(joined, inc=1, device_id={"tp": LEADER}, device_id_type=MESH)

    def pair_copy(place):
        return pltpu.make_async_remote_copy(
            src_ref=pair_out.at[place], dst_ref=pair_in.at[place],
            send_sem=pair_send.at[place], recv_sem=pair_recv.at[place],
            device_id={"tp": partner}, device_id_type=MESH,
        )

    def line_copy(way, place, h, to):
        rows = pl.ds(h * PIECE, PIECE)
        return pltpu.make_async_remote_copy(
            src_ref=line_out.at[place, rows], dst_ref=landing.at[way, place, rows],
            send_sem=line_send.at[place, h], recv_sem=line_recv.at[way, place, h],
            device_id={"tp": to}, device_id_type=MESH,
        )

    def block(place, h):
        rows = pl.ds(h * PIECE, PIECE)
        return own[place, rows] + pair_in[place, rows].astype(F32)

    def multiply_pair(step):
        place, head = head_of(step, 1 - core)
        pair_out[pl.ds(place, 1)] = dot(scaled[...], head_weight(head)).astype(BF16)[None]
        if step == 0:
            @pl.when(tp == LEADER)
            def _():
                pl.semaphore_wait(joined, TP - 1)
                lax.fori_loop(1, GRP, greet_leaders, 0)
        pair_copy(place).start()

    def multiply_own(step):
        place, head = head_of(step, core)
        own[pl.ds(place, 1)] = dot(scaled[...], head_weight(head))[None]

    def first_sends(step):
        place, _ = head_of(step, 0)
        way = chip // (CHIPS - 1)

        @pl.when(chip % (CHIPS - 1) == 0)
        def _():
            pair_copy(place).wait_recv()
            for h in range(PIECES):
                rows = pl.ds(h * PIECE, PIECE)
                line_out[place, rows] = block(place, h).astype(BF16)
                line_copy(way, place, h, tp + 2 - 4 * way).start()

    for load in later_loads:
        load.start()

    def square_copy(i):
        return pltpu.make_async_remote_copy(
            src_ref=squares.at[tp], dst_ref=squares.at[tp],
            send_sem=sq_send.at[i], recv_sem=sq_recv.at[tp],
            device_id={"tp": (tp + i) % TP}, device_id_type=MESH,
        )

    def square_arrival(i):
        source = (tp + i) % TP
        return pltpu.make_async_remote_copy(
            src_ref=squares.at[source], dst_ref=squares.at[source],
            send_sem=sq_send.at[i], recv_sem=sq_recv.at[source],
            device_id={"tp": source}, device_id_type=MESH,
        )

    for chunk in range(CHUNKS):
        load_weight(chunk).wait()
    multiply_pair(0)
    multiply_own(0)
    first_sends(0)
    multiply_pair(1)
    for h in range(2):
        floats = tokens[pl.ds(h * HALF, HALF), :].astype(F32)
        square = floats * floats
        high = square.astype(BF16)
        low = (square - high.astype(F32)).astype(BF16)
        ones = jnp.ones((8, FEATS), BF16)
        sums = dot(ones, high, NT) + dot(ones, low, NT)
        squares[pl.ds(tp, 1), :, h * HALF:(h + 1) * HALF] = sums[0:1, :].reshape(1, 1, HALF)
    for i in range(1, TP):
        square_copy(i).start()
    multiply_pair(2)
    multiply_own(1)
    first_sends(1)
    multiply_pair(3)
    multiply_own(2)
    first_sends(2)
    multiply_own(3)

    for load in later_loads:
        load.wait()
    lengths = lengths_ref[...]
    dests = dest_ref[...]
    mine = iota((GRP, GRP), 0) == group
    own_lengths = jnp.sum(jnp.where(mine, lengths, 0), axis=0, keepdims=True)
    own_dest = jnp.sum(jnp.where(mine, dests, 0), axis=0, keepdims=True)
    before = (iota((GRP, GRP), 0) < iota((GRP, GRP), 1)).astype(F32)
    spread = jnp.broadcast_to(own_lengths.astype(F32), (8, GRP))
    starts = dot(spread, before)[0:1, :].astype(jnp.int32)
    by_layer = iota((GRP, GRP), 0) % PLANE * LAYERS + iota((GRP, GRP), 0) // PLANE
    routed = own_dest == by_layer
    slot_first = jnp.sum(jnp.where(routed, starts, 0), axis=1, keepdims=True)
    slot_length = jnp.sum(jnp.where(routed, own_lengths, 0), axis=1, keepdims=True)
    for part in range(8):
        requests = slice(part * 8, part * 8 + 8)
        offset = iota((8, SLOT, ROWS), 1)
        first = slot_first[requests][:, :, None]
        length = slot_length[requests][:, :, None]
        hit = (iota((8, SLOT, ROWS), 2) == first + offset) & (offset < length)
        pick[part // 2, part % 2 * 128:part % 2 * 128 + 128, :] = hit.astype(F32).reshape(128, ROWS).astype(BF16)

    row_index = iota((ROWS, GRP), 0)
    first_row = jnp.max(jnp.where(starts <= row_index, starts, 0), axis=1, keepdims=True)
    at_offset = (iota((ROWS, SLOT), 1) + first_row == iota((ROWS, SLOT), 0)).astype(F32).astype(BF16)
    rest = table_ref[...]
    tabled = jnp.zeros((ROWS, 2 * HD), F32)
    for _ in range(3):
        term = rest.astype(BF16)
        rest = rest - term.astype(F32)
        tabled = tabled + dot(at_offset, term)
    cos_rows[...] = tabled[:, 0:HD]
    sin_rows[...] = tabled[:, HD:2 * HD]

    live_rows = jnp.sum(jnp.where(dests == group, lengths, 0), axis=1, keepdims=True)
    for z in range(LAYERS):
        at_source = iota((GRP, LANES), 1) // SLOT * LAYERS + z == iota((GRP, LANES), 0)
        live_lanes = jnp.sum(jnp.where(at_source, live_rows, 0), axis=0, keepdims=True)
        live[z] = (iota((1, LANES), 1) % SLOT < live_lanes).astype(F32)

    sorted_row = iota((4 * GRP, 4 * GRP), 0)
    natural = (sorted_row // 4 % PLANE * LAYERS + sorted_row // (4 * PLANE)) * 4 + sorted_row % 4
    column = iota((4 * GRP, 4 * GRP), 1)
    new_keys[...] = dot((column == natural).astype(F32).astype(BF16), new_ref[...]).astype(BF16)
    shifted = (column == natural + 2) & (sorted_row % 4 < 2)
    new_values[...] = dot(shifted.astype(F32).astype(BF16), new_ref[...]).astype(BF16)

    scale = 1.0 / math.sqrt(HD)
    same = iota((128, 128), 0) // 16 == iota((128, 128), 1) // 16
    same_new = (iota((128, 32), 0) // 16 == iota((128, 32), 1) // 4) & (iota((128, 32), 1) % 4 <= iota((128, 32), 0) % 2)
    for z in range(LAYERS):
        for half in range(2):
            eight = slice(half * 8, half * 8 + 8)
            asked = query[z, eight].reshape(128, HD)
            cached_keys = old[z, eight, :, 0:HD].reshape(128, HD)
            fresh_keys = new_keys[z * 64 + half * 32:z * 64 + half * 32 + 32, :]
            score_old[2 * z + half] = jnp.where(same, dot(asked, cached_keys, NT) * scale, -1e30)
            score_new[2 * z + half] = jnp.where(same_new, dot(asked, fresh_keys, NT) * scale, -1e30)

    def schedule(here):
        events = []
        for way in range(2):
            from_end = here if way == 0 else CHIPS - 1 - here
            for back in range(CHIPS - 1):
                place = CHIPS - 1 - back if way == 0 else back
                if from_end and (place >= here if way == 0 else place <= here):
                    for h in range(PIECES):
                        sent = back * PIECES + h + 1
                        events.append((sent + from_end * LAG + (from_end - 1), way, place, h))
        return [event[1:] for event in sorted(events)]

    schedules = {here: schedule(here) for here in range(CHIPS)}
    have = {0: {3, 2, 1}, 1: set(), 2: set(), 3: {0, 1, 2}}
    begun = {here: set() for here in range(CHIPS)}

    def follow(here, events):
        for way, place, h in events:
            if place not in have[here]:
                have[here].add(place)
                pair_copy(place).wait_recv()
            rows = pl.ds(h * PIECE, PIECE)
            value = final[rows, :] if place == here and h in begun[here] else block(place, h)
            line_copy(way, place, h, tp + 4 * way - 2).wait_recv()
            value = value + landing[way, place, rows].astype(F32)
            if place == here:
                begun[here].add(h)
                final[rows, :] = value
            else:
                line_out[place, rows] = value.astype(BF16)
                line_copy(way, place, h, tp + 2 - 4 * way).start()

    def finish(rows):
        inverse = inverse_rms[rows, :]
        keys = final[rows, 0:HD] * inverse + bias_ref[0:HD][None, :]
        values = final[rows, HD:WIDTH] * inverse + bias_ref[HD:WIDTH][None, :]
        turned = pltpu.roll(keys, HD // 2, 1)
        handed[rows, 0:HD] = (keys * cos_rows[rows, :] + turned * sin_rows[rows, :]).astype(BF16)
        handed[rows, HD:WIDTH] = values.astype(BF16)

    @pl.when(tp == LEADER)
    def _():
        pl.semaphore_wait(barrier, GRP - 1)
        lax.fori_loop(1, TP, tell_group, 0)

    for here in range(CHIPS):
        pl.when(chip == here)(functools.partial(follow, here, schedules[here][:-1]))
    for i in range(1, TP):
        square_arrival(i).wait_recv()
    total = jnp.sum(squares[...].reshape(TP, ROWS), axis=0, keepdims=True)
    inverse_rms[...] = jnp.broadcast_to(lax.rsqrt(total / D + EPSILON), (HD, ROWS)).T
    finish(pl.ds(0, ROWS - PIECE))
    for z in range(LAYERS):
        early[z] = dot(pick[z, :, 0:ROWS - PIECE], handed[0:ROWS - PIECE, :])

    @pl.when(tp != LEADER)
    def _():
        pl.semaphore_wait(all_in, 1)

    for here in range(CHIPS):
        pl.when(chip == here)(functools.partial(follow, here, schedules[here][-1:]))
    finish(pl.ds(ROWS - PIECE, PIECE))

    y, x = plane // 4, plane % 4

    def send(aways):
        def body(i, carry):
            target = (y + i // 4) % 4 * 4 + (x + i % 4) % 4
            for away in aways:
                target_layer = (layer + away) % LAYERS
                copy = pltpu.make_async_remote_copy(
                    src_ref=outgoing.at[target_layer, target], dst_ref=arrived.at[layer, plane],
                    send_sem=hand_send.at[away], recv_sem=hand_recv.at[away],
                    device_id={"grp": target * LAYERS + target_layer}, device_id_type=MESH,
                )
                if away:
                    copy.start()
                else:
                    pl.when(i > 0)(copy.start)
            return carry
        return body

    def handed_over(away):
        blocks = pl.ds(0, PLANE if away else PLANE - 1)
        return pltpu.make_async_remote_copy(
            src_ref=outgoing.at[0, blocks], dst_ref=arrived.at[0, blocks],
            send_sem=hand_send.at[away], recv_sem=hand_recv.at[away],
            device_id={"grp": (group + 1) % GRP}, device_id_type=MESH,
        )

    for aways in ((1, 3), (2,), (0,)):
        for away in aways:
            target_layer = (layer + away) % LAYERS
            late = dot(pick[target_layer, :, ROWS - PIECE:ROWS], handed[ROWS - PIECE:ROWS, :])
            picked = (early[target_layer] + late).astype(BF16)
            outgoing[pl.ds(target_layer, 1)] = picked.reshape(1, PLANE, SLOT, WIDTH)
        lax.fori_loop(0, PLANE, send(aways), 0)
    arrived[pl.ds(layer, 1), pl.ds(plane, 1)] = outgoing[pl.ds(layer, 1), pl.ds(plane, 1)]

    for away in (0, 1, 3, 2):
        handed_over(away).wait_recv()
        z = (layer + LAYERS - away) % LAYERS
        span_live = live[z] > 0.5
        for half in range(2):
            eight = pl.ds(half * 8, 8)
            asked = query[z, eight].reshape(128, HD)
            old_values = old[z, eight, :, HD:WIDTH].reshape(128, HD)
            span_keys = arrived[z, eight, :, 0:HD].reshape(128, HD)
            span_values = arrived[z, eight, :, HD:WIDTH].reshape(128, HD)
            fresh_values = new_values[pl.ds(pl.multiple_of(z * 64 + half * 32, 32), 32), :]
            cached, fresh = score_old[2 * z + half], score_new[2 * z + half]
            may = same & span_live[:, half * 128:half * 128 + 128]
            span = jnp.where(may, dot(asked, span_keys, NT) * scale, -1e30)
            top = jnp.max(jnp.maximum(cached, span), axis=1, keepdims=True)
            top = jnp.maximum(top, jnp.max(fresh, axis=1, keepdims=True))
            cached, span, fresh = jnp.exp(cached - top), jnp.exp(span - top), jnp.exp(fresh - top)
            weight_sum = jnp.sum(cached + span, axis=1, keepdims=True) + jnp.sum(fresh, axis=1, keepdims=True)
            inverse = 1.0 / weight_sum
            result = dot((cached * inverse).astype(BF16), old_values)
            result = result + dot((span * inverse).astype(BF16), span_values)
            result = result + dot((fresh * inverse).astype(BF16), fresh_values)
            out_ref[eight, pl.ds(z, 1)] = result.astype(BF16).reshape(8, 1, SLOT, HD)

    for place in range(CHIPS):
        pair_copy(place).wait_send()
        for h in range(PIECES):
            @pl.when(chip != place)
            def _(place=place, h=h):
                line_copy(0, place, h, partner).wait_send()
    for i in range(1, TP):
        square_copy(i).wait_send()
    for away in (0, 1, 3, 2):
        handed_over(away).wait_send()


def shards(tokens, gain, kv_weight, kv_bias, lengths, dest, queries, old_cache, new_kv):
    query_rows = queries.reshape(GRP, STEPS, QPK, HD).transpose(0, 2, 1, 3).reshape(PLANE, LAYERS, SLOT, HD)
    new_rows = new_kv.reshape(GRP, STEPS, 2, HD).transpose(0, 2, 1, 3).reshape(4 * GRP, HD)
    vmem = pl.BlockSpec(memory_space=pltpu.VMEM)
    dma = pltpu.SemaphoreType.DMA
    out = pl.pallas_call(
        kernel,
        out_shape=jax.ShapeDtypeStruct((PLANE, LAYERS, SLOT, HD), BF16),
        in_specs=[pl.BlockSpec(memory_space=pltpu.HBM)] * 10,
        out_specs=vmem,
        scratch_shapes=[
            pltpu.VMEM((ROWS, FEATS), BF16),
            pltpu.VMEM((ROWS, FEATS), BF16),
            pltpu.VMEM((FEATS, KVW), BF16),
            pltpu.VMEM((FEATS,), F32),
            pltpu.VMEM((WIDTH,), F32),
            pltpu.VMEM((GRP, GRP), jnp.int32),
            pltpu.VMEM((GRP, GRP), jnp.int32),
            pltpu.VMEM((LAYERS, PLANE, SLOT, HD), BF16),
            pltpu.VMEM((LAYERS, PLANE, SLOT, WIDTH), BF16),
            pltpu.VMEM((4 * GRP, HD), BF16),
            pltpu.VMEM((4 * GRP, HD), BF16),
            pltpu.VMEM((4 * GRP, HD), BF16),
            pltpu.VMEM((SLOT, 2 * HD), F32),
            pltpu.VMEM((CHIPS, ROWS, WIDTH), BF16),
            pltpu.VMEM((CHIPS, ROWS, WIDTH), BF16),
            pltpu.VMEM((CHIPS, ROWS, WIDTH), F32),
            pltpu.VMEM((2, CHIPS, ROWS, WIDTH), BF16),
            pltpu.VMEM((CHIPS, ROWS, WIDTH), BF16),
            pltpu.VMEM((ROWS, WIDTH), F32),
            pltpu.VMEM((ROWS, WIDTH), BF16),
            pltpu.VMEM((LAYERS, LANES, WIDTH), F32),
            pltpu.VMEM((TP, 1, ROWS), F32),
            pltpu.VMEM((LAYERS, LANES, ROWS), BF16),
            pltpu.VMEM((ROWS, HD), F32),
            pltpu.VMEM((ROWS, HD), F32),
            pltpu.VMEM((ROWS, HD), F32),
            pltpu.VMEM((LAYERS, 1, LANES), F32),
            pltpu.VMEM((8, 128, 128), F32),
            pltpu.VMEM((8, 128, 32), F32),
            pltpu.VMEM((LAYERS, PLANE, SLOT, WIDTH), BF16),
            pltpu.VMEM((LAYERS, PLANE, SLOT, WIDTH), BF16),
            pltpu.SemaphoreType.REGULAR,
            pltpu.SemaphoreType.REGULAR,
            dma((15,)),
            dma((CHUNKS,)),
            dma((TP,)),
            dma((TP,)),
            dma((CHIPS,)),
            dma((CHIPS,)),
            dma((CHIPS, PIECES)),
            dma((2, CHIPS, PIECES)),
            dma((LAYERS,)),
            dma((LAYERS,)),
        ],
        compiler_params=pltpu.CompilerParams(
            collective_id=0, has_side_effects=True, vmem_limit_bytes=40 * 1024 * 1024
        ),
        cost_estimate=pl.CostEstimate(flops=2_500_000_000, bytes_accessed=6_000_000, transcendentals=300_000),
    )(
        *(
            pltpu.with_memory_space_constraint(operand, pltpu.HBM)
            for operand in (
                tokens, kv_weight, gain, kv_bias, lengths, dest,
                query_rows, old_cache.reshape(PLANE, LAYERS, SLOT, WIDTH), new_rows, jnp.asarray(rotary_tables()),
            )
        )
    )
    return out.reshape(GRP, QPK, STEPS, HD).transpose(0, 2, 1, 3).reshape(1, GRP, STEPS, QPK * HD)


def solution(mesh):
    return jax.shard_map(
        shards,
        mesh=mesh,
        in_specs=(
            P("grp", "tp"),
            P("tp"),
            P("tp", None),
            P("tp"),
            P(),
            P(),
            P("grp", None, None, "tp"),
            P("grp", None, None, "tp"),
            P("grp", None, None, "tp"),
        ),
        out_specs=P("grp", None, None, "tp"),
        check_vma=False,
    )
```
